256 devices in a mesh: ens: 16 (over x_lo, z), mesh: 16 (over y, x_hi, core).
Axes of the slice: x: 4 (x_hi: 2, x_lo: 2; x = x_hi * 2 + x_lo), y: 4, z: 8, core: 2. Of those that a mesh axis runs over, the one named last changes fastest.
Arguments:
- inputs: bfloat16 [16, 4096, 512], P('ens', 'mesh'), may hold values from -6 to 6
- cotangent: bfloat16 [16, 4096, 512], P('ens', 'mesh'), may hold values from -6 to 6
- noise_level: float32 [16], P('ens'), may hold values from 0.02 to 80
- neighbours: int32 [4096, 32], P('mesh'), may hold values from 0 to 4095, as said below
- live_slots: int32 [4096, 32], P('mesh'), may hold values from 0 to 1
- projections: bfloat16 [2, 4, 512, 512], replicated, may hold values from -4 to 4
- film_weights: float32 [2, 32, 1024], replicated, may hold values from -0.5 to 0.5
Outputs:
- grad_input: bfloat16 [16, 4096, 512], P('ens', 'mesh')
- grad_projections: float32 [2, 4, 512, 512], P(None, None, 'ens', 'mesh')
- grad_film: float32 [2, 32, 1024], P(None, None, 'mesh')
The draws below stay inside these ranges and needn't reach their ends.
Inputs may be any that keep to these rules, and one draw needn't show every extreme that they name: `neighbours`: slot 0 of node i names i and is live. The live slots of a node name distinct nodes within 128 of it; every node at least 128 from both ends of the numbering has a live slot exactly 128 away. Padded slots name the node itself.
All inputs are finite; a program needn't handle non-finite values.
Results may differ from the reference program's by a relative error of at most 0.028.
Values may be sent and summed in bfloat16 or wider, within the bound.
A program may use at most 64 MiB of HBM per device.

```python
import math
import jax
import jax.numpy as jnp
from jax import lax

D = 512
HEADS = 4
HEAD = 128
SLOTS = 32
NOISE_FREQ = 16
LAYERS = 2
REACH = 128
MEMBERS = 16
NODES = 4096


def graph_tables(key):
    node_ids = jnp.arange(NODES)[:, None]
    candidates = jnp.concatenate([jnp.arange(-REACH, 0), jnp.arange(1, REACH + 1)])
    score_key, side_key, count_key = jax.random.split(jax.random.fold_in(key, 7), 3)
    raw_scores = jax.random.randint(score_key, (NODES, 2 * REACH), 0, 1 << 20)
    rank_scores = raw_scores * (2 * REACH) + jnp.arange(2 * REACH)[None, :]
    far_side = jax.random.randint(side_key, (NODES,), 0, 2)
    far_slot = jnp.where(far_side == 0, 0, 2 * REACH - 1)
    rank_scores = jnp.where(jnp.arange(2 * REACH)[None, :] == far_slot[:, None], 1 << 30, rank_scores)
    picked = lax.top_k(rank_scores, SLOTS - 1)[1]
    offsets = jnp.concatenate([jnp.zeros((NODES, 1), jnp.int32), candidates[picked].astype(jnp.int32)], axis=1)
    targets = node_ids + offsets
    inside = (targets >= 0) & (targets < NODES)
    counts = jax.random.randint(count_key, (NODES, 1), SLOTS // 2, SLOTS + 1)
    live_flags = inside & (jnp.arange(SLOTS)[None, :] < counts)
    neighbours = jnp.where(live_flags, targets, node_ids)
    return (neighbours.astype(jnp.int32), live_flags.astype(jnp.int32))


def draw_neighbours(key, part):
    return graph_tables(key)[0]


def draw_live_slots(key, part):
    return graph_tables(key)[1]


def draw_projections(key, part):
    base_key = jax.random.fold_in(jax.random.fold_in(key, 11), 0)
    base_draw = jax.random.normal(base_key, (LAYERS, 4, D, D), jnp.float32) / math.sqrt(D)
    return jnp.clip(base_draw, -4.0, 4.0).astype(jnp.bfloat16)


def steps_of(own_key, dims, cuts, smallest, high):
    level = 1.0
    for dim, blocks in cuts:
        draws = jax.random.uniform(jax.random.fold_in(jax.random.fold_in(own_key, 6), dim), (blocks,), jnp.float32, smallest / len(cuts), high / len(cuts))
        level = level * jnp.repeat(jnp.exp(draws), dims[dim] // blocks).reshape((-1,) + (1,) * (len(dims) - 1 - dim))
    return level


def scatter_about(own_key, dims, width, limit, cuts=(), held_as=jnp.bfloat16):
    factor_of = steps_of(own_key, dims, cuts, -0.22, 0.18) if cuts else 1.0
    values = jax.random.normal(own_key, dims, jnp.float32) * width * factor_of
    return jnp.minimum(jnp.maximum(values, -limit), limit).astype(held_as)


def setup_inputs(seed: int = 0) -> dict:
    keys = jax.random.split(jax.random.key(seed), 8)
    return {
        "inputs": scatter_about(keys[0], (MEMBERS, NODES, D), 1.0, 6.0, ((0, 16), (1, 16))),
        "cotangent": scatter_about(keys[1], (MEMBERS, NODES, D), 1.0, 6.0, ((0, 16), (1, 16))),
        "noise_level": jnp.clip(jnp.exp(math.log(80.0) - 8.2940497 * jax.random.uniform(keys[2], (MEMBERS,), jnp.float32) ** steps_of(keys[2], (MEMBERS,), ((0, 16),), -0.2, 0.2)), 0.02, 80.0),
        "neighbours": draw_neighbours(jax.random.fold_in(keys[7], 71), 0),
        "live_slots": draw_live_slots(jax.random.fold_in(keys[7], 71), 0),
        "projections": draw_projections(jax.random.fold_in(keys[7], 71), 0),
        "film_weights": scatter_about(keys[6], (LAYERS, 2 * NOISE_FREQ, 2 * D), 0.1, 0.5, (), jnp.float32),
    }


epsilon = 1e-05

def noise_features(noise_level):
    frequency = jnp.arange(1, NOISE_FREQ + 1).astype(jnp.float32)
    angles = jnp.log(noise_level)[:, None] * frequency[None, :]
    return jnp.concatenate([jnp.sin(angles), jnp.cos(angles)], axis=1)

def project(left_side, right_side):
    return jnp.dot(left_side, right_side, preferred_element_type=jnp.float32)

def contract_rows(left_side, right_side):
    return lax.dot_general(left_side, right_side, (((0,), (0,)), ((), ())), preferred_element_type=jnp.float32)

def contract_cols(left_side, right_side):
    return lax.dot_general(left_side, right_side, (((1,), (1,)), ((), ())), preferred_element_type=jnp.float32)

def normalize(states, film_row):
    values = states.astype(jnp.float32)
    centre = lax.optimization_barrier(jnp.mean(values, axis=1, keepdims=True))
    spread = lax.optimization_barrier(jnp.mean(jnp.square(values - centre), axis=1, keepdims=True))
    inverse = lax.rsqrt(spread + epsilon)
    unit_rows = (values - centre) * inverse
    normed = (unit_rows * (1.0 + film_row[:D]) + film_row[D:]).astype(jnp.bfloat16)
    return (unit_rows, inverse, normed)

def gather_heads(rows, neighbours, head_index):
    return rows[:, head_index * HEAD:(head_index + 1) * HEAD][neighbours].astype(jnp.float32)

def slot_attention(query_head, key_slots, live_mask):
    scores = jnp.einsum('nc,nsc->ns', query_head, key_slots) / math.sqrt(HEAD)
    scores = jnp.where(live_mask, scores, -jnp.inf)
    row_peak = lax.optimization_barrier(jnp.max(scores, axis=1, keepdims=True))
    weights = jnp.where(live_mask, jnp.exp(scores - row_peak), 0.0)
    return weights / lax.optimization_barrier(jnp.sum(weights, axis=1, keepdims=True))

def forward_layer(states, film_row, weights, neighbours, live_mask):
    unit_rows, inverse, normed = normalize(states, film_row)
    queries = project(normed, weights[0]).astype(jnp.bfloat16)
    key_rows = project(normed, weights[1]).astype(jnp.bfloat16)
    value_rows = project(normed, weights[2]).astype(jnp.bfloat16)
    pieces = []
    for head_index in range(HEADS):
        head_cols = slice(head_index * HEAD, (head_index + 1) * HEAD)
        attention = slot_attention(queries[:, head_cols].astype(jnp.float32), gather_heads(key_rows, neighbours, head_index), live_mask)
        rounded = lax.optimization_barrier(attention.astype(jnp.bfloat16)).astype(jnp.float32)
        pieces.append(jnp.einsum('ns,nsc->nc', rounded, gather_heads(value_rows, neighbours, head_index)))
    attended = jnp.concatenate(pieces, axis=1).astype(jnp.bfloat16)
    outputs = (states.astype(jnp.float32) + project(attended, weights[3])).astype(jnp.bfloat16)
    return (outputs, (unit_rows, inverse, normed, queries, key_rows, value_rows, attended))

def backward_layer(upstream, film_row, weights, stored, neighbours, live_mask):
    unit_rows, inverse, normed, queries, key_rows, value_rows, attended = stored
    node_count = upstream.shape[0]
    grad_out = contract_rows(attended, upstream)
    grad_attended = contract_cols(upstream, weights[3]).astype(jnp.bfloat16)
    query_parts, key_parts, value_parts = ([], [], [])
    for head_index in range(HEADS):
        head_cols = slice(head_index * HEAD, (head_index + 1) * HEAD)
        key_slots = gather_heads(key_rows, neighbours, head_index)
        value_slots = gather_heads(value_rows, neighbours, head_index)
        query_head = queries[:, head_cols].astype(jnp.float32)
        attention = slot_attention(query_head, key_slots, live_mask)
        rounded = lax.optimization_barrier(attention.astype(jnp.bfloat16)).astype(jnp.float32)
        grad_head = grad_attended[:, head_cols].astype(jnp.float32)
        grad_probs = jnp.einsum('nc,nsc->ns', grad_head, value_slots)
        grad_scores = attention * (grad_probs - lax.optimization_barrier(jnp.sum(attention * grad_probs, axis=1, keepdims=True))) / math.sqrt(HEAD)
        grad_scores = lax.optimization_barrier(grad_scores.astype(jnp.bfloat16)).astype(jnp.float32)
        query_parts.append(jnp.einsum('ns,nsc->nc', grad_scores, key_slots))
        key_terms = grad_scores[:, :, None] * query_head[:, None, :]
        key_parts.append(jnp.zeros((node_count, HEAD), jnp.float32).at[neighbours].add(key_terms))
        value_terms = rounded[:, :, None] * grad_head[:, None, :]
        value_parts.append(jnp.zeros((node_count, HEAD), jnp.float32).at[neighbours].add(value_terms))
    grad_queries = jnp.concatenate(query_parts, axis=1).astype(jnp.bfloat16)
    grad_keys = jnp.concatenate(key_parts, axis=1).astype(jnp.bfloat16)
    grad_values = jnp.concatenate(value_parts, axis=1).astype(jnp.bfloat16)
    grad_weights = jnp.stack([contract_rows(normed, grad_queries), contract_rows(normed, grad_keys), contract_rows(normed, grad_values), grad_out])
    grad_normed = contract_cols(grad_queries, weights[0]) + contract_cols(grad_keys, weights[1]) + contract_cols(grad_values, weights[2])
    grad_conditioning = jnp.concatenate([lax.optimization_barrier(jnp.sum(grad_normed * unit_rows, axis=0)), lax.optimization_barrier(jnp.sum(grad_normed, axis=0))])
    grad_unit = grad_normed * (1.0 + film_row[:D])
    centred = grad_unit - lax.optimization_barrier(jnp.mean(grad_unit, axis=1, keepdims=True)) - unit_rows * lax.optimization_barrier(jnp.mean(grad_unit * unit_rows, axis=1, keepdims=True))
    new_upstream = (upstream.astype(jnp.float32) + inverse * centred).astype(jnp.bfloat16)
    return (new_upstream, grad_weights, grad_conditioning)

def member_pass(states, cotangent, embedding, projections, film_weights, neighbours, live_mask):
    film_rows = [jnp.dot(embedding[None, :], film_weights[layer_number], precision=lax.Precision.HIGHEST)[0] for layer_number in range(LAYERS)]
    stored = []
    current = states
    for layer_number in range(LAYERS):
        current, saved = forward_layer(current, film_rows[layer_number], projections[layer_number], neighbours, live_mask)
        stored.append(saved)
    upstream = cotangent
    weight_list = [None] * LAYERS
    film_list = [None] * LAYERS
    for layer_number in reversed(range(LAYERS)):
        upstream, grad_weights, grad_conditioning = backward_layer(upstream, film_rows[layer_number], projections[layer_number], stored[layer_number], neighbours, live_mask)
        weight_list[layer_number] = grad_weights
        film_list[layer_number] = embedding[:, None] * grad_conditioning[None, :]
    return (upstream, jnp.stack(weight_list), jnp.stack(film_list))

def reference(inputs, cotangent, noise_level, neighbours, live_slots, projections, film_weights):
    embeddings = noise_features(noise_level)
    live_mask = live_slots > 0

    def per_member(bundle):
        return member_pass(bundle[0], bundle[1], bundle[2], projections, film_weights, neighbours, live_mask)
    grad_input, weight_all, film_all = lax.map(per_member, (inputs, cotangent, embeddings))
    return (grad_input, lax.optimization_barrier(jnp.sum(weight_all, axis=0)), lax.optimization_barrier(jnp.sum(film_all, axis=0)))
```

```python
import functools
import math

import jax
import jax.numpy as jnp
from jax import lax
from jax.experimental import pallas as pl
from jax.experimental.pallas import tpu as pltpu
from jax.sharding import PartitionSpec as P

HEADS = 4
NOISE_FREQ = 16
LAYERS = 2
EPSILON = 1e-05
MESH = pl.DeviceIdType.MESH
F32 = jnp.float32
BF16 = jnp.bfloat16
REACH = 128
WIN = 3 * REACH
D = 512
HEAD = D // HEADS
SCALE = 1.0 / math.sqrt(HEAD)


def noise_features(noise_level):
    frequency = jnp.arange(1, NOISE_FREQ + 1).astype(jnp.float32)
    angles = jnp.log(noise_level)[:, None] * frequency[None, :]
    return jnp.concatenate([jnp.sin(angles), jnp.cos(angles)], axis=1)


def nn(a, b):
    return lax.dot_general(a, b, (((1,), (0,)), ((), ())), preferred_element_type=F32)


def nt(a, b):
    return lax.dot_general(a, b, (((1,), (1,)), ((), ())), preferred_element_type=F32)


def kernel(
    ne, nm,
    x_ref, cot_ref, emb_ref, nb_ref, live_ref, w_hbm, fw_ref,
    gin_ref, gw_ref, gf_ref,
    w_v, hx1, hx2, hcot, hup, x2, up1, normed, unit, inv, qe, ke, ve, gae, prob, att,
    bias, bias_t, nl_pad, nl_own, nl_halo, nl_all, stat, stat_own, stat_halo,
    dq, dk, dv, wb, rc, s2, r2, acc, s3, r3, cond, rcond, s2f, r2f, s3f, r3f,
    w_sem, hs_sem, hr_sem, cs_sem, cr_sem, s2_sem, r2_sem, s3_sem, r3_sem,
):
    nq = nm // 2
    cw = D // nm
    rw = D // ne
    e = lax.axis_index("ens")
    m = lax.axis_index("mesh")
    q = m // 2
    core = m % 2
    right = (m + 1) % nm
    left = (m + nm - 1) % nm
    partner = m + 1 - 2 * core
    base = m * (2 * REACH)

    w_copies = {}
    for layer in range(LAYERS):
        for mat in range(4):
            c = pltpu.make_async_copy(w_hbm.at[layer, mat], w_v.at[layer, mat], w_sem.at[layer, mat])
            c.start()
            w_copies[layer, mat] = c

    barrier = pltpu.get_barrier_semaphore()

    def greet(em, mm):
        pl.semaphore_signal(barrier, inc=1, device_id=(em, mm), device_id_type=MESH)

    greet(e, left)
    greet(e, right)
    for k in range(1, nq):
        greet(e, ((q + k) % nq) * 2 + core)
    for k in range(1, ne):
        greet((e + k) % ne, m)
    pl.semaphore_wait(barrier, 2 + (nq - 1) + (ne - 1))

    def rcopy(src, dst, ssem, rsem, em, mm):
        c = pltpu.make_async_remote_copy(
            src_ref=src, dst_ref=dst, send_sem=ssem, recv_sem=rsem, device_id=(em, mm), device_id_type=MESH
        )
        c.start()
        return c

    def halo(kind, low, high, dst):
        a = rcopy(high, dst.at[0], hs_sem.at[kind, 0], hr_sem.at[kind, 0], e, right)
        b = rcopy(low, dst.at[1], hs_sem.at[kind, 1], hr_sem.at[kind, 1], e, left)
        return (a, b)

    def wait_recv(pair):
        for c in pair:
            c.wait_recv()

    sent = []
    LOW, HIGH = pl.ds(0, REACH), pl.ds(REACH, REACH)
    h_x1 = halo(0, x_ref.at[0, LOW], x_ref.at[0, HIGH], hx1)

    nl_pad[...] = jnp.zeros_like(nl_pad)
    nl_pad[:, 0:32] = jnp.where(live_ref[...] > 0, nb_ref[...], -100000).astype(F32)
    for half in range(2):
        nl_own[half] = nl_pad[half * REACH:(half + 1) * REACH, :].T[0:32]
    h_nl = halo(1, nl_own.at[0], nl_own.at[1], nl_halo)
    h_cot = halo(2, cot_ref.at[0, LOW], cot_ref.at[0, HIGH], hcot)
    stat[...] = jnp.zeros_like(stat)
    cond[...] = jnp.zeros_like(cond)
    s3f[...] = jnp.zeros_like(s3f)

    emb = emb_ref[...]
    scales, shifts = [], []
    for layer in range(LAYERS):
        pieces = [
            jnp.sum(emb * fw_ref[layer, :, g * 128:(g + 1) * 128], axis=0, keepdims=True) for g in range(8)
        ]
        row = jnp.concatenate(pieces, axis=1)
        scales.append(1.0 + row[:, :D])
        shifts.append(row[:, D:])

    def normalize(states, layer):
        values = states.astype(F32)
        centre = jnp.mean(values, axis=1, keepdims=True)
        off = values - centre
        spread = jnp.mean(off * off, axis=1, keepdims=True)
        inverse = lax.rsqrt(spread + EPSILON)
        u = off * inverse
        return u, inverse, (u * scales[layer] + shifts[layer]).astype(BF16)

    def project_rows(rows, n, layer):
        w = w_v.at[layer]
        qe[layer, rows] = nn(n, w[0]).astype(BF16)
        ke[layer, rows] = nn(n, w[1]).astype(BF16)
        ve[layer, rows] = nn(n, w[2]).astype(BF16)

    def own_rows(src, layer):
        def step(i, carry):
            rows = pl.ds(pl.multiple_of(i * 64, 64), 64)
            u, inverse, n = normalize(src[rows], layer)
            unit[layer, rows] = u
            inv[layer, rows] = jnp.broadcast_to(inverse, (64, 128))
            normed[layer, rows] = n
            return carry

        lax.fori_loop(0, 4, step, 0)
        project_rows(pl.ds(REACH, 2 * REACH), normed[layer], layer)

    def halo_rows(src, layer):
        for side in range(2):
            _, _, n = normalize(src[side], layer)
            project_rows(pl.ds(side * 3 * REACH, REACH), n, layer)

    def attend(layer):
        for b in range(2):
            rows = pl.ds(REACH + b * REACH, REACH)
            window = pl.ds(b * REACH, WIN)
            for h in range(HEADS):
                cols = slice(h * HEAD, (h + 1) * HEAD)
                s = nt(qe[layer, rows, cols], ke[layer, window, cols]) * SCALE + bias[b]
                peak = jnp.max(s, axis=1, keepdims=True)
                wts = jnp.exp(s - peak)
                total = jnp.sum(wts, axis=1, keepdims=True)
                p = wts * (1.0 / total)
                prob[layer, b * HEADS + h] = p
                stat[layer, b * REACH:(b + 1) * REACH, h:h + 1] = peak + jnp.log(total)
                att[layer, b * REACH:(b + 1) * REACH, cols] = nn(
                    p.astype(BF16), ve[layer, window, cols]
                ).astype(BF16)

    def mask_step(i, carry):
        rows = pl.ds(pl.multiple_of(i * 32, 32), 32)
        first = base - REACH + (i // 4) * REACH
        jid = (lax.broadcasted_iota(jnp.int32, (32, WIN), 1) + first).astype(F32)
        table = nl_pad[rows, 0:32]
        out = jnp.full((32, WIN), -jnp.inf, F32)
        for s in range(32):
            out = jnp.where(table[:, s:s + 1] == jid, 0.0, out)
        bias[i // 4, pl.ds(pl.multiple_of((i % 4) * 32, 32), 32)] = out
        return carry

    for mat in range(3):
        w_copies[0, mat].wait()
    own_rows(x_ref.at[0], 0)
    lax.fori_loop(0, 8, mask_step, 0)
    wait_recv(h_x1)
    halo_rows(hx1, 0)
    attend(0)
    w_copies[0, 3].wait()
    x2[...] = (x_ref[0].astype(F32) + nn(att[0], w_v[0, 3])).astype(BF16)
    h_x2 = halo(3, x2.at[LOW], x2.at[HIGH], hx2)
    for mat in range(4):
        w_copies[1, mat].wait()
    own_rows(x2, 1)

    wait_recv(h_nl)
    nl_all[0] = nl_halo[0]
    nl_all[1] = nl_own[0]
    nl_all[2] = nl_own[1]
    nl_all[3] = nl_halo[1]

    def mask_t_step(i, carry):
        jb = i // 2
        rows = (i % 2) * 64
        jid = (lax.broadcasted_iota(jnp.int32, (64, 128), 0) + (base + jb * REACH + rows)).astype(F32)
        for t in range(3):
            table = nl_all[jb + t]
            out = jnp.full((64, 128), -jnp.inf, F32)
            for s in range(32):
                out = jnp.where(table[s:s + 1, :] == jid, 0.0, out)
            bias_t[jb, pl.ds(pl.multiple_of(rows, 64), 64), t * 128:(t + 1) * 128] = out
        return carry

    lax.fori_loop(0, 4, mask_t_step, 0)

    def grad_attended(up_own, up_halo, layer, which):
        w3 = w_v[layer, 3]
        if which != 1:
            gae[pl.ds(REACH, 2 * REACH)] = nt(up_own, w3).astype(BF16)
        if which != 0:
            for side in range(2):
                gae[pl.ds(side * 3 * REACH, REACH)] = nt(up_halo[side], w3).astype(BF16)

    wait_recv(h_cot)
    grad_attended(cot_ref[0], hcot, 1, 2)
    wait_recv(h_x2)
    halo_rows(hx2, 1)
    attend(1)

    def query_pass(layer):
        for b in range(2):
            rows = pl.ds(REACH + b * REACH, REACH)
            window = pl.ds(b * REACH, WIN)
            for h in range(HEADS):
                cols = slice(h * HEAD, (h + 1) * HEAD)
                gp = nt(gae[rows, cols], ve[layer, window, cols])
                p = prob[layer, b * HEADS + h]
                delta = jnp.sum(p * gp, axis=1, keepdims=True)
                stat[layer, b * REACH:(b + 1) * REACH, HEADS + h:HEADS + h + 1] = delta
                gs = (p * ((gp - delta) * SCALE)).astype(BF16)
                dq[b * REACH:(b + 1) * REACH, cols] = nn(gs, ke[layer, window, cols]).astype(BF16)
        for half in range(2):
            stat_own[layer, half] = stat[layer, half * REACH:(half + 1) * REACH, :].T[0:8]
        return halo(5 + layer, stat_own.at[layer, 0], stat_own.at[layer, 1], stat_halo.at[layer])

    def key_pass(layer):
        for jb in range(2):
            rows = pl.ds(REACH + jb * REACH, REACH)
            window = pl.ds(jb * REACH, WIN)
            if jb == 0:
                parts = [stat_halo[layer, 0], stat_own[layer, 0], stat_own[layer, 1]]
            else:
                parts = [stat_own[layer, 0], stat_own[layer, 1], stat_halo[layer, 1]]
            stats = jnp.concatenate(parts, axis=1)
            for h in range(HEADS):
                cols = slice(h * HEAD, (h + 1) * HEAD)
                queries = qe[layer, window, cols]
                grads = gae[window, cols]
                s = nt(ke[layer, rows, cols], queries) * SCALE + bias_t[jb]
                p = jnp.exp(s - stats[h:h + 1])
                gp = nt(ve[layer, rows, cols], grads)
                gs = (p * ((gp - stats[HEADS + h:HEADS + h + 1]) * SCALE)).astype(BF16)
                dk[jb * REACH:(jb + 1) * REACH, cols] = nn(gs, queries).astype(BF16)
                dv[jb * REACH:(jb + 1) * REACH, cols] = nn(p.astype(BF16), grads).astype(BF16)

    def weight_grad(batch, t, left_side, right_side):
        per = 128 // cw

        def step(cb, carry):
            a = left_side[:, pl.ds(pl.multiple_of(cb * 128, 128), 128)]
            res = nn(a.T, right_side[...]).astype(BF16)
            for u in range(per):
                piece = res[u * cw:(u + 1) * cw]
                if per == 1:
                    wb[batch, cb % 2, t, cb // 2] = piece
                else:
                    wb[batch, u % 2, t, cb * (per // 2) + u // 2] = piece
            return carry

        lax.fori_loop(0, 4, step, 0)

    def start_core(batch):
        return rcopy(wb.at[batch, 1 - core], rc.at[batch], cs_sem.at[batch], cr_sem.at[batch], e, partner)

    def core_sum(batch, copy):
        copy.wait_recv()

        def step(i, carry):
            for t in range(2):
                s2[batch, i, t] = (wb[batch, core, t, i].astype(F32) + rc[batch, t, i].astype(F32)).astype(BF16)
            return carry

        lax.fori_loop(0, nq, step, 0)
        copies = []
        for k in range(1, nq):
            peer = (q + k) % nq
            copies.append(
                rcopy(
                    s2.at[batch, peer], r2.at[batch, k], s2_sem.at[batch, k], r2_sem.at[batch, k],
                    e, peer * 2 + core,
                )
            )
        return copies

    def chip_sum(batch, copies):
        for c in copies:
            c.wait_recv()
        for t in range(2):
            total = s2[batch, q, t].astype(F32)
            for k in range(1, nq):
                total = total + r2[batch, k, t].astype(F32)
            first = ((batch % 2) * 2 + t) * cw
            acc[batch // 2, first:first + cw] = total

    def start_ens(slot):
        whole = acc[slot].T.astype(BF16)
        for i in range(ne):
            s3[slot, i] = whole[i * rw:(i + 1) * rw]
        copies = []
        for k in range(1, ne):
            peer = (e + k) % ne
            copies.append(
                rcopy(s3.at[slot, peer], r3.at[slot, k], s3_sem.at[slot, k], r3_sem.at[slot, k], peer, m)
            )
        return copies

    def ens_sum(slot, copies, layer):
        for c in copies:
            c.wait_recv()
        total = s3[slot, e].astype(F32)
        for k in range(1, ne):
            total = total + r3[slot, k].astype(F32)
        for pos, mat in enumerate((3, 0, 1, 2)):
            gw_ref[layer, mat] = total[:, pos * cw:(pos + 1) * cw]

    def input_pass(layer, up, out):
        w = w_v.at[layer]

        def step(i, carry):
            first, second = carry
            rows = pl.ds(pl.multiple_of(i * 128, 128), 128)
            gn = nt(dq[rows], w[0]) + nt(dk[rows], w[1]) + nt(dv[rows], w[2])
            u = unit[layer, rows]
            gu = gn * u
            first = first + jnp.sum(gu, axis=0, keepdims=True)
            second = second + jnp.sum(gn, axis=0, keepdims=True)
            g = gn * scales[layer]
            mean_g = jnp.mean(g, axis=1, keepdims=True)
            mean_gu = jnp.mean(g * u, axis=1, keepdims=True)
            centred = g - mean_g - u * mean_gu
            out[rows] = (up[rows].astype(F32) + inv[layer, rows][:, 0:1] * centred).astype(BF16)
            return (first, second)

        zero = jnp.zeros((1, D), F32)
        first, second = lax.fori_loop(0, 2, step, (zero, zero))
        row = jnp.concatenate([first, second], axis=1)
        width = 2 * D // nq
        for i in range(nq):
            cond[i, layer:layer + 1] = row[:, i * width:(i + 1) * width]

    st = query_pass(1)
    sent.extend(st)
    weight_grad(0, 0, cot_ref.at[0], att.at[1])
    weight_grad(0, 1, dq, normed.at[1])
    core0 = start_core(0)
    wait_recv(st)
    key_pass(1)
    input_pass(1, cot_ref.at[0], up1)
    h_up = halo(4, up1.at[LOW], up1.at[HIGH], hup)
    weight_grad(1, 0, dk, normed.at[1])
    weight_grad(1, 1, dv, normed.at[1])
    core1 = start_core(1)
    chips0 = core_sum(0, core0)
    grad_attended(up1[...], hup, 0, 0)
    wait_recv(h_up)
    grad_attended(up1, hup, 0, 1)

    st = query_pass(0)
    sent.extend(st)
    chips1 = core_sum(1, core1)
    weight_grad(2, 0, up1, att.at[0])
    weight_grad(2, 1, dq, normed.at[0])
    core2 = start_core(2)
    wait_recv(st)
    key_pass(0)
    chips2 = core_sum(2, core2)
    weight_grad(3, 0, dk, normed.at[0])
    weight_grad(3, 1, dv, normed.at[0])
    core3 = start_core(3)
    input_pass(0, up1, gin_ref.at[0])
    core_f = rcopy(cond, rcond, cs_sem.at[4], cr_sem.at[4], e, partner)
    chips3 = core_sum(3, core3)
    core_f.wait_recv()
    s2f[...] = cond[...] + rcond[...]
    chips_f = []
    for k in range(1, nq):
        peer = (q + k) % nq
        chips_f.append(
            rcopy(s2f.at[peer], r2f.at[k], s2_sem.at[4, k], r2_sem.at[4, k], e, peer * 2 + core)
        )
    chip_sum(0, chips0)
    chip_sum(1, chips1)
    ens_b = start_ens(0)
    for c in chips_f:
        c.wait_recv()
    total = s2f[q]
    for k in range(1, nq):
        total = total + r2f[k]
    s3f[...] = total
    eye = lax.broadcasted_iota(jnp.int32, (32, 128), 0) == lax.broadcasted_iota(jnp.int32, (32, 128), 1)
    s3f[2:3, 0:128] = jnp.sum(jnp.where(eye, emb, 0.0), axis=0, keepdims=True)
    ens_f = []
    for k in range(1, ne):
        ens_f.append(rcopy(s3f, r3f.at[k], s3_sem.at[2, k], r3_sem.at[2, k], (e + k) % ne, m))
    chip_sum(2, chips2)
    chip_sum(3, chips3)
    ens_a = start_ens(1)

    for c in ens_f:
        c.wait_recv()
    films = [None] * LAYERS
    for k in range(ne):
        tile = s3f[...] if k == 0 else r3f[k]
        column = jnp.sum(jnp.where(eye, tile[2:3, 0:128], 0.0), axis=1, keepdims=True)
        for layer in range(LAYERS):
            part = column * tile[layer:layer + 1]
            films[layer] = part if films[layer] is None else films[layer] + part
    half = D // nq
    for layer in range(LAYERS):
        gf_ref[layer] = jnp.where(core == 0, films[layer][:, :half], films[layer][:, half:])
    ens_sum(0, ens_b, 1)
    ens_sum(1, ens_a, 0)

    for pair in (h_x1, h_nl, h_cot, h_x2, h_up):
        sent.extend(pair)
    sent.extend([core0, core1, core2, core3, core_f])
    for group in (chips0, chips1, chips2, chips3, chips_f, ens_a, ens_b, ens_f):
        sent.extend(group)
    for c in sent:
        c.wait_send()


def body(ne, nm, inputs, cotangent, noise_level, neighbours, live_slots, projections, film_weights):
    emb = noise_features(noise_level)[0]
    emb = jnp.broadcast_to(emb[:, None], (2 * NOISE_FREQ, 128))
    nq, cw, rw, fl = nm // 2, D // nm, D // ne, 4 * D // nm
    own = 2 * REACH
    vm = pl.BlockSpec(memory_space=pltpu.VMEM)
    V = pltpu.VMEM
    scratch = [
        V((LAYERS, 4, D, D), BF16),
        V((2, REACH, D), BF16), V((2, REACH, D), BF16), V((2, REACH, D), BF16), V((2, REACH, D), BF16),
        V((own, D), BF16), V((own, D), BF16),
        V((LAYERS, own, D), BF16), V((LAYERS, own, D), F32), V((LAYERS, own, 128), F32),
        V((LAYERS, 2 * own, D), BF16), V((LAYERS, 2 * own, D), BF16), V((LAYERS, 2 * own, D), BF16),
        V((2 * own, D), BF16),
        V((LAYERS, 2 * HEADS, REACH, WIN), F32), V((LAYERS, own, D), BF16),
        V((2, REACH, WIN), F32), V((2, REACH, WIN), F32),
        V((own, 128), F32), V((2, 32, 128), F32), V((2, 32, 128), F32), V((4, 32, 128), F32),
        V((LAYERS, own, 128), F32), V((LAYERS, 2, 8, 128), F32), V((LAYERS, 2, 8, 128), F32),
        V((own, D), BF16), V((own, D), BF16), V((own, D), BF16),
        V((4, 2, 2, nq, cw, D), BF16), V((4, 2, nq, cw, D), BF16),
        V((4, nq, 2, cw, D), BF16), V((4, nq, 2, cw, D), BF16),
        V((2, 4 * cw, D), F32), V((2, ne, rw, 4 * cw), BF16), V((2, ne, rw, 4 * cw), BF16),
        V((nq, 8, fl), F32), V((nq, 8, fl), F32), V((nq, 8, fl), F32), V((nq, 8, fl), F32),
        V((8, fl), F32), V((ne, 8, fl), F32),
        pltpu.SemaphoreType.DMA((LAYERS, 4)),
        pltpu.SemaphoreType.DMA((7, 2)), pltpu.SemaphoreType.DMA((7, 2)),
        pltpu.SemaphoreType.DMA((5,)), pltpu.SemaphoreType.DMA((5,)),
        pltpu.SemaphoreType.DMA((5, nq)), pltpu.SemaphoreType.DMA((5, nq)),
        pltpu.SemaphoreType.DMA((3, ne)), pltpu.SemaphoreType.DMA((3, ne)),
    ]
    return pl.pallas_call(
        functools.partial(kernel, ne, nm),
        out_shape=(
            jax.ShapeDtypeStruct((1, own, D), BF16),
            jax.ShapeDtypeStruct((LAYERS, 4, rw, cw), F32),
            jax.ShapeDtypeStruct((LAYERS, 2 * NOISE_FREQ, fl // 2), F32),
        ),
        in_specs=[vm, vm, vm, vm, vm, pl.BlockSpec(memory_space=pl.ANY), vm],
        out_specs=(vm, vm, vm),
        scratch_shapes=scratch,
        compiler_params=pltpu.CompilerParams(
            collective_id=0, has_side_effects=True, vmem_limit_bytes=56 * 1024 * 1024
        ),
    )(inputs, cotangent, emb, neighbours, live_slots, projections, film_weights)


def solution(mesh):
    placed = (
        P("ens", "mesh", None),
        P("ens", "mesh", None),
        P("ens"),
        P("mesh", None),
        P("mesh", None),
        P(),
        P(),
    )
    return jax.shard_map(
        functools.partial(body, mesh.shape["ens"], mesh.shape["mesh"]),
        mesh=mesh,
        in_specs=placed,
        out_specs=(P("ens", "mesh", None), P(None, None, "ens", "mesh"), P(None, None, "mesh")),
        check_vma=False,
    )
```

```python
import functools
import math

import jax
import jax.numpy as jnp
from jax import lax
from jax.experimental import pallas as pl
from jax.experimental.pallas import tpu as pltpu
from jax.sharding import PartitionSpec as P

HEADS = 4
NOISE_FREQ = 16
LAYERS = 2
EPSILON = 1e-05
MESH = pl.DeviceIdType.MESH
F32 = jnp.float32
BF16 = jnp.bfloat16
REACH = 128
WIN = 3 * REACH
D = 512
HEAD = D // HEADS
SCALE = 1.0 / math.sqrt(HEAD)
SCALE2 = SCALE * math.log2(math.e)


def noise_features(noise_level):
    frequency = jnp.arange(1, NOISE_FREQ + 1).astype(jnp.float32)
    angles = jnp.log(noise_level)[:, None] * frequency[None, :]
    return jnp.concatenate([jnp.sin(angles), jnp.cos(angles)], axis=1)


def nn(a, b):
    return lax.dot_general(a, b, (((1,), (0,)), ((), ())), preferred_element_type=F32)


def nt(a, b):
    return lax.dot_general(a, b, (((1,), (1,)), ((), ())), preferred_element_type=F32)


def kernel(
    ne, nm,
    x_ref, cot_ref, emb_ref, nb_ref, live_ref, w_hbm, fw_ref,
    gin_ref, gw_ref, gf_ref,
    w_v, hx1, hx2, hcot, hup, x2, up1, normed, unit, inv, qe, ke, ve, gae, prob, att,
    bias, bias_t, nl_own, nl_halo, stat, stat_own, stat_halo,
    dq, dk, dv, wb, rc, s2, r2, acc, s3, r3, cond, rcond, s2f, r2f, s3f, r3f,
    w_sem, hs_sem, hr_sem, cs_sem, cr_sem, s2_sem, r2_sem, s3_sem, r3_sem,
):
    nq = nm // 2
    cw = D // nm
    rw = D // ne
    e = lax.axis_index("ens")
    m = lax.axis_index("mesh")
    q = m // 2
    core = m % 2
    right = (m + 1) % nm
    left = (m + nm - 1) % nm
    partner = m + 1 - 2 * core
    base = m * (2 * REACH)

    w_copies = {}
    for layer in range(LAYERS):
        for mat in range(4):
            c = pltpu.make_async_copy(w_hbm.at[layer, mat], w_v.at[layer, mat], w_sem.at[layer, mat])
            c.start()
            w_copies[layer, mat] = c

    barrier = pltpu.get_barrier_semaphore()

    def greet(em, mm):
        pl.semaphore_signal(barrier, inc=1, device_id=(em, mm), device_id_type=MESH)

    greet(e, left)
    greet(e, right)
    for k in range(1, nq):
        greet(e, ((q + k) % nq) * 2 + core)
    for k in range(1, ne):
        greet((e + k) % ne, m)
    pl.semaphore_wait(barrier, 2 + (nq - 1) + (ne - 1))

    def rcopy(src, dst, ssem, rsem, em, mm):
        c = pltpu.make_async_remote_copy(
            src_ref=src, dst_ref=dst, send_sem=ssem, recv_sem=rsem, device_id=(em, mm), device_id_type=MESH
        )
        c.start()
        return c

    def halo(kind, low, high, dst):
        a = rcopy(high, dst.at[0], hs_sem.at[kind, 0], hr_sem.at[kind, 0], e, right)
        b = rcopy(low, dst.at[1], hs_sem.at[kind, 1], hr_sem.at[kind, 1], e, left)
        return (a, b)

    def wait_recv(pair):
        for c in pair:
            c.wait_recv()

    sent = []
    LOW, HIGH = pl.ds(0, REACH), pl.ds(REACH, REACH)
    h_x1 = halo(0, x_ref.at[0, LOW], x_ref.at[0, HIGH], hx1)

    table = jnp.where(live_ref[...] > 0, nb_ref[...], -100000).astype(F32)
    for half in range(2):
        nl_own[half] = table[:, half * REACH:(half + 1) * REACH]
    h_nl = halo(1, nl_own.at[0], nl_own.at[1], nl_halo)
    stat[...] = jnp.zeros_like(stat)
    cond[...] = jnp.zeros_like(cond)
    s3f[...] = jnp.zeros_like(s3f)

    emb = emb_ref[...]
    scales, shifts = [], []
    for layer in range(LAYERS):
        pieces = [
            jnp.sum(emb * fw_ref[layer, :, g * 128:(g + 1) * 128], axis=0, keepdims=True) for g in range(8)
        ]
        row = jnp.concatenate(pieces, axis=1)
        scales.append(1.0 + row[:, :D])
        shifts.append(row[:, D:])

    def normalize(states, layer):
        values = states.astype(F32)
        centre = jnp.mean(values, axis=1, keepdims=True)
        off = values - centre
        spread = jnp.mean(off * off, axis=1, keepdims=True)
        inverse = lax.rsqrt(spread + EPSILON)
        u = off * inverse
        return u, inverse, (u * scales[layer] + shifts[layer]).astype(BF16)

    def project_rows(rows, n, layer):
        w = w_v.at[layer]
        qe[layer, rows] = nn(n, w[0]).astype(BF16)
        ke[layer, rows] = nn(n, w[1]).astype(BF16)
        ve[layer, rows] = nn(n, w[2]).astype(BF16)

    def own_rows(src, layer):
        def step(i, carry):
            rows = pl.ds(pl.multiple_of(i * 64, 64), 64)
            u, inverse, n = normalize(src[rows], layer)
            unit[layer, rows] = u
            inv[layer, rows] = jnp.broadcast_to(inverse, (64, 128))
            normed[layer, rows] = n
            return carry

        lax.fori_loop(0, 4, step, 0)
        project_rows(pl.ds(REACH, 2 * REACH), normed[layer], layer)

    def halo_rows(src, layer):
        for side in range(2):
            _, _, n = normalize(src[side], layer)
            project_rows(pl.ds(side * 3 * REACH, REACH), n, layer)

    def attend(layer):
        for b in range(2):
            rows = pl.ds(REACH + b * REACH, REACH)
            window = pl.ds(b * REACH, WIN)
            for h in range(HEADS):
                cols = slice(h * HEAD, (h + 1) * HEAD)
                s = nt(qe[layer, rows, cols], ke[layer, window, cols]) * SCALE2 + bias[b]
                peak = jnp.max(s, axis=1, keepdims=True)
                wts = jnp.exp2(s - peak)
                total = jnp.sum(wts, axis=1, keepdims=True)
                p = wts * (1.0 / total)
                prob[layer, b * HEADS + h] = p
                stat[layer, b * REACH:(b + 1) * REACH, h:h + 1] = peak + jnp.log2(total)
                att[layer, b * REACH:(b + 1) * REACH, cols] = nn(
                    p.astype(BF16), ve[layer, window, cols]
                ).astype(BF16)

    def mask_tile(table, first):
        jid = (lax.broadcasted_iota(jnp.int32, (REACH, REACH), 0) + first).astype(F32)
        out = jnp.full((REACH, REACH), -jnp.inf, F32)
        for s in range(32):
            out = jnp.where(table[s:s + 1, :] == jid, 0.0, out)
        return out

    def own_masks():
        for b in range(2):
            for t in range(3):
                tile = mask_tile(nl_own[b], base + (b + t - 1) * REACH)
                jb = b + t - 1
                if 0 <= jb <= 1:
                    place = b + 1 - jb
                    bias_t[jb, :, place * REACH:(place + 1) * REACH] = tile
                bias[b, :, t * REACH:(t + 1) * REACH] = tile.T

    def halo_masks():
        bias_t[0, :, 0:REACH] = mask_tile(nl_halo[0], base)
        bias_t[1, :, 2 * REACH:] = mask_tile(nl_halo[1], base + REACH)

    for mat in range(3):
        w_copies[0, mat].wait()
    own_rows(x_ref.at[0], 0)
    own_masks()
    wait_recv(h_x1)
    h_cot = halo(2, cot_ref.at[0, LOW], cot_ref.at[0, HIGH], hcot)
    halo_rows(hx1, 0)
    attend(0)
    w_copies[0, 3].wait()
    x2[...] = (x_ref[0].astype(F32) + nn(att[0], w_v[0, 3])).astype(BF16)
    h_x2 = halo(3, x2.at[LOW], x2.at[HIGH], hx2)
    for mat in range(4):
        w_copies[1, mat].wait()
    own_rows(x2, 1)

    wait_recv(h_nl)
    halo_masks()

    def grad_attended(up_own, up_halo, layer, which):
        w3 = w_v[layer, 3]
        if which != 1:
            gae[pl.ds(REACH, 2 * REACH)] = nt(up_own, w3).astype(BF16)
        if which != 0:
            for side in range(2):
                gae[pl.ds(side * 3 * REACH, REACH)] = nt(up_halo[side], w3).astype(BF16)

    wait_recv(h_cot)
    grad_attended(cot_ref[0], hcot, 1, 2)
    wait_recv(h_x2)
    halo_rows(hx2, 1)
    attend(1)

    def query_pass(layer):
        for b in range(2):
            rows = pl.ds(REACH + b * REACH, REACH)
            window = pl.ds(b * REACH, WIN)
            for h in range(HEADS):
                cols = slice(h * HEAD, (h + 1) * HEAD)
                gp = nt(gae[rows, cols], ve[layer, window, cols])
                p = prob[layer, b * HEADS + h]
                delta = jnp.sum(p * gp, axis=1, keepdims=True)
                stat[layer, b * REACH:(b + 1) * REACH, HEADS + h:HEADS + h + 1] = delta
                gs = (p * ((gp - delta) * SCALE)).astype(BF16)
                dq[b * REACH:(b + 1) * REACH, cols] = nn(gs, ke[layer, window, cols]).astype(BF16)
        for half in range(2):
            stat_own[layer, half] = stat[layer, half * REACH:(half + 1) * REACH, :].T[0:8]
        return halo(5 + layer, stat_own.at[layer, 0], stat_own.at[layer, 1], stat_halo.at[layer])

    def key_pass(layer):
        for jb in range(2):
            rows = pl.ds(REACH + jb * REACH, REACH)
            window = pl.ds(jb * REACH, WIN)
            if jb == 0:
                parts = [stat_halo[layer, 0], stat_own[layer, 0], stat_own[layer, 1]]
            else:
                parts = [stat_own[layer, 0], stat_own[layer, 1], stat_halo[layer, 1]]
            stats = jnp.concatenate(parts, axis=1)
            for h in range(HEADS):
                cols = slice(h * HEAD, (h + 1) * HEAD)
                queries = qe[layer, window, cols]
                grads = gae[window, cols]
                s = nt(ke[layer, rows, cols], queries) * SCALE2 + bias_t[jb]
                p = jnp.exp2(s - stats[h:h + 1])
                gp = nt(ve[layer, rows, cols], grads)
                gs = (p * ((gp - stats[HEADS + h:HEADS + h + 1]) * SCALE)).astype(BF16)
                dk[jb * REACH:(jb + 1) * REACH, cols] = nn(gs, queries).astype(BF16)
                dv[jb * REACH:(jb + 1) * REACH, cols] = nn(p.astype(BF16), grads).astype(BF16)

    def weight_grad(batch, left_side, right_side):
        res = nn(left_side[...].T, right_side[...]).astype(BF16)
        for i in range(nm):
            wb[batch, i % 2, i // 2] = res[i * cw:(i + 1) * cw]
        return rcopy(wb.at[batch, 1 - core], rc.at[batch], cs_sem.at[batch], cr_sem.at[batch], e, partner)

    def core_sum(batch, copy):
        copy.wait_recv()
        copies = []
        for k in range(nq):
            peer = (q + k) % nq
            s2[batch, peer] = (wb[batch, core, peer].astype(F32) + rc[batch, peer].astype(F32)).astype(BF16)
            if k > 0:
                copies.append(
                    rcopy(
                        s2.at[batch, peer], r2.at[batch, k], s2_sem.at[batch, k], r2_sem.at[batch, k],
                        e, peer * 2 + core,
                    )
                )
        return copies

    def chip_sum(batch, copies):
        for c in copies:
            c.wait_recv()
        total = s2[batch, q].astype(F32)
        for k in range(1, nq):
            total = total + r2[batch, k].astype(F32)
        first = (batch % 4) * cw
        acc[batch // 4, first:first + cw] = total

    def start_ens(slot):
        whole = acc[slot].T.astype(BF16)
        for i in range(ne):
            s3[slot, i] = whole[i * rw:(i + 1) * rw]
        copies = []
        for k in range(1, ne):
            peer = (e + k) % ne
            copies.append(
                rcopy(s3.at[slot, peer], r3.at[slot, k], s3_sem.at[slot, k], r3_sem.at[slot, k], peer, m)
            )
        return copies

    def ens_sum(slot, copies, layer):
        for c in copies:
            c.wait_recv()
        total = s3[slot, e].astype(F32)
        for k in range(1, ne):
            total = total + r3[slot, k].astype(F32)
        for pos, mat in enumerate((3, 0, 1, 2)):
            gw_ref[layer, mat] = total[:, pos * cw:(pos + 1) * cw]

    def input_rows(layer, up, out, i):
        w = w_v.at[layer]
        rows = pl.ds(i * REACH, REACH)
        gn = nt(dq[rows], w[0]) + nt(dk[rows], w[1]) + nt(dv[rows], w[2])
        u = unit[layer, rows]
        gu = gn * u
        first = jnp.sum(gu, axis=0, keepdims=True)
        second = jnp.sum(gn, axis=0, keepdims=True)
        mean_g = jnp.mean(gn * scales[layer], axis=1, keepdims=True)
        mean_gu = jnp.mean(gu * scales[layer], axis=1, keepdims=True)
        centred = gn * scales[layer] - mean_g - u * mean_gu
        out[rows] = (up[rows].astype(F32) + inv[layer, rows][:, 0:1] * centred).astype(BF16)
        return jnp.concatenate([first, second], axis=1)

    def put_cond(layer, row):
        width = 2 * D // nq
        for i in range(nq):
            cond[i, layer:layer + 1] = row[:, i * width:(i + 1) * width]

    core_l2o = weight_grad(0, cot_ref.at[0], att.at[1])
    st = query_pass(1)
    sent.extend(st)
    core_l2q = weight_grad(1, dq, normed.at[1])
    chips = {}
    chips[0] = core_sum(0, core_l2o)
    wait_recv(st)
    key_pass(1)
    row = input_rows(1, cot_ref.at[0], up1, 0)
    up_a = rcopy(up1.at[LOW], hup.at[1], hs_sem.at[4, 1], hr_sem.at[4, 1], e, left)
    row = row + input_rows(1, cot_ref.at[0], up1, 1)
    up_b = rcopy(up1.at[HIGH], hup.at[0], hs_sem.at[4, 0], hr_sem.at[4, 0], e, right)
    put_cond(1, row)
    core_l2k = weight_grad(2, dk, normed.at[1])
    core_l2v = weight_grad(3, dv, normed.at[1])
    chips[1] = core_sum(1, core_l2q)
    core_l1o = weight_grad(4, up1, att.at[0])
    grad_attended(up1[...], hup, 0, 0)

    st = query_pass(0)
    sent.extend(st)
    wait_recv((up_a, up_b))
    grad_attended(up1, hup, 0, 1)
    core_l1q = weight_grad(5, dq, normed.at[0])
    chips[2] = core_sum(2, core_l2k)
    chips[3] = core_sum(3, core_l2v)
    wait_recv(st)
    key_pass(0)
    core_l1k = weight_grad(6, dk, normed.at[0])
    core_l1v = weight_grad(7, dv, normed.at[0])
    chips[4] = core_sum(4, core_l1o)
    chips[5] = core_sum(5, core_l1q)
    row = input_rows(0, up1, gin_ref.at[0], 0)
    chips[6] = core_sum(6, core_l1k)
    row = row + input_rows(0, up1, gin_ref.at[0], 1)
    put_cond(0, row)
    core_f = rcopy(cond, rcond, cs_sem.at[8], cr_sem.at[8], e, partner)
    chips[7] = core_sum(7, core_l1v)
    for i in range(4):
        chip_sum(i, chips[i])
    ens_b = start_ens(0)
    core_f.wait_recv()
    s2f[...] = cond[...] + rcond[...]
    chips_f = []
    for k in range(1, nq):
        peer = (q + k) % nq
        chips_f.append(
            rcopy(s2f.at[peer], r2f.at[k], s2_sem.at[8, k], r2_sem.at[8, k], e, peer * 2 + core)
        )
    for c in chips_f:
        c.wait_recv()
    total = s2f[q]
    for k in range(1, nq):
        total = total + r2f[k]
    s3f[...] = total
    eye = lax.broadcasted_iota(jnp.int32, (32, 128), 0) == lax.broadcasted_iota(jnp.int32, (32, 128), 1)
    s3f[2:3, 0:128] = jnp.sum(jnp.where(eye, emb, 0.0), axis=0, keepdims=True)
    ens_f = []
    for k in range(1, ne):
        ens_f.append(rcopy(s3f, r3f.at[k], s3_sem.at[2, k], r3_sem.at[2, k], (e + k) % ne, m))
    for i in range(4, 8):
        chip_sum(i, chips[i])
    ens_a = start_ens(1)

    for c in ens_f:
        c.wait_recv()
    films = [None] * LAYERS
    for k in range(ne):
        tile = s3f[...] if k == 0 else r3f[k]
        column = jnp.sum(jnp.where(eye, tile[2:3, 0:128], 0.0), axis=1, keepdims=True)
        for layer in range(LAYERS):
            part = column * tile[layer:layer + 1]
            films[layer] = part if films[layer] is None else films[layer] + part
    half = D // nq
    for layer in range(LAYERS):
        gf_ref[layer] = jnp.where(core == 0, films[layer][:, :half], films[layer][:, half:])
    ens_sum(0, ens_b, 1)
    ens_sum(1, ens_a, 0)

    for pair in (h_x1, h_nl, h_cot, h_x2, (up_a, up_b)):
        sent.extend(pair)
    sent.extend([core_l2o, core_l2q, core_l2k, core_l2v, core_l1o, core_l1q, core_l1k, core_l1v, core_f])
    for group in [chips[i] for i in range(8)] + [chips_f, ens_a, ens_b, ens_f]:
        sent.extend(group)
    for c in sent:
        c.wait_send()


def hand_over(a_ref, b_ref, c_ref, a_out, b_out, c_out):
    a_out[...] = a_ref[...]
    b_out[...] = b_ref[...]
    c_out[...] = c_ref[...]


def body(ne, nm, inputs, cotangent, noise_level, neighbours, live_slots, projections, film_weights):
    emb = noise_features(noise_level)[0]
    emb = jnp.broadcast_to(emb[:, None], (2 * NOISE_FREQ, 128))
    nq, cw, rw, fl = nm // 2, D // nm, D // ne, 4 * D // nm
    own = 2 * REACH
    vm = pl.BlockSpec(memory_space=pltpu.VMEM)
    V = pltpu.VMEM
    scratch = [
        V((LAYERS, 4, D, D), BF16),
        V((2, REACH, D), BF16), V((2, REACH, D), BF16), V((2, REACH, D), BF16), V((2, REACH, D), BF16),
        V((own, D), BF16), V((own, D), BF16),
        V((LAYERS, own, D), BF16), V((LAYERS, own, D), F32), V((LAYERS, own, 128), F32),
        V((LAYERS, 2 * own, D), BF16), V((LAYERS, 2 * own, D), BF16), V((LAYERS, 2 * own, D), BF16),
        V((2 * own, D), BF16),
        V((LAYERS, 2 * HEADS, REACH, WIN), F32), V((LAYERS, own, D), BF16),
        V((2, REACH, WIN), F32), V((2, REACH, WIN), F32),
        V((2, 32, 128), F32), V((2, 32, 128), F32),
        V((LAYERS, own, 128), F32), V((LAYERS, 2, 8, 128), F32), V((LAYERS, 2, 8, 128), F32),
        V((own, D), BF16), V((own, D), BF16), V((own, D), BF16),
        V((8, 2, nq, cw, D), BF16), V((8, nq, cw, D), BF16),
        V((8, nq, cw, D), BF16), V((8, nq, cw, D), BF16),
        V((2, 4 * cw, D), F32), V((2, ne, rw, 4 * cw), BF16), V((2, ne, rw, 4 * cw), BF16),
        V((nq, 8, fl), F32), V((nq, 8, fl), F32), V((nq, 8, fl), F32), V((nq, 8, fl), F32),
        V((8, fl), F32), V((ne, 8, fl), F32),
        pltpu.SemaphoreType.DMA((LAYERS, 4)),
        pltpu.SemaphoreType.DMA((7, 2)), pltpu.SemaphoreType.DMA((7, 2)),
        pltpu.SemaphoreType.DMA((9,)), pltpu.SemaphoreType.DMA((9,)),
        pltpu.SemaphoreType.DMA((9, nq)), pltpu.SemaphoreType.DMA((9, nq)),
        pltpu.SemaphoreType.DMA((3, ne)), pltpu.SemaphoreType.DMA((3, ne)),
    ]
    outs = pl.pallas_call(
        functools.partial(kernel, ne, nm),
        out_shape=(
            jax.ShapeDtypeStruct((1, own, D), BF16),
            jax.ShapeDtypeStruct((LAYERS, 4, rw, cw), F32),
            jax.ShapeDtypeStruct((LAYERS, 2 * NOISE_FREQ, fl // 2), F32),
        ),
        in_specs=[vm, vm, vm, vm, vm, pl.BlockSpec(memory_space=pl.ANY), vm],
        out_specs=(vm, vm, vm),
        scratch_shapes=scratch,
        compiler_params=pltpu.CompilerParams(
            collective_id=0, has_side_effects=True, vmem_limit_bytes=56 * 1024 * 1024
        ),
    )(inputs, cotangent, emb, neighbours.T, live_slots.T, projections, film_weights)
    return pl.pallas_call(
        hand_over,
        out_shape=tuple(jax.ShapeDtypeStruct(o.shape, o.dtype) for o in outs),
        in_specs=[vm, vm, vm],
        out_specs=(vm, vm, vm),
    )(*outs)


def solution(mesh):
    placed = (
        P("ens", "mesh", None),
        P("ens", "mesh", None),
        P("ens"),
        P("mesh", None),
        P("mesh", None),
        P(),
        P(),
    )
    return jax.shard_map(
        functools.partial(body, mesh.shape["ens"], mesh.shape["mesh"]),
        mesh=mesh,
        in_specs=placed,
        out_specs=(P("ens", "mesh", None), P(None, None, "ens", "mesh"), P(None, None, "mesh")),
        check_vma=False,
    )
```

```python
import functools
import math

import jax
import jax.numpy as jnp
from jax import lax
from jax.experimental import pallas as pl
from jax.experimental.pallas import tpu as pltpu
from jax.sharding import PartitionSpec as P

HEADS = 4
NOISE_FREQ = 16
LAYERS = 2
EPSILON = 1e-05
MESH = pl.DeviceIdType.MESH
F32 = jnp.float32
BF16 = jnp.bfloat16
REACH = 128
WIN = 3 * REACH
D = 512
HEAD = D // HEADS
SCALE = 1.0 / math.sqrt(HEAD)
SCALE2 = SCALE * math.log2(math.e)


def noise_features(noise_level):
    frequency = jnp.arange(1, NOISE_FREQ + 1).astype(jnp.float32)
    angles = jnp.log(noise_level)[:, None] * frequency[None, :]
    return jnp.concatenate([jnp.sin(angles), jnp.cos(angles)], axis=1)


def nn(a, b):
    return lax.dot_general(a, b, (((1,), (0,)), ((), ())), preferred_element_type=F32)


def nt(a, b):
    return lax.dot_general(a, b, (((1,), (1,)), ((), ())), preferred_element_type=F32)


def kernel(
    ne, nm,
    x_ref, cot_ref, emb_ref, nb_ref, live_ref, w_hbm, fw_ref,
    gin_ref, gw_ref, gf_ref,
    w_v, hx1, hx2, hcot, hup, x2, up1, normed, unit, inv, qe, ke, ve, gae, prob, att,
    bias, bias_t, nl_own, nl_halo, stat, stat_own, stat_halo,
    dq, dk, dv, wb, rc, s2, r2, t2, rt, acc, s3, r3, cond, rcond, s2f, ryf, sxf, rxf, s3f, r3f,
    w_sem, hs_sem, hr_sem, cs_sem, cr_sem, s2_sem, r2_sem, t2_sem, rt_sem, s3_sem, r3_sem,
):
    nq = nm // 2
    cw = D // nm
    rw = D // ne
    e = lax.axis_index("ens")
    m = lax.axis_index("mesh")
    ny, nz = nm // 4, ne // 2
    core = m % 2
    y = m // 4
    z = e % nz
    x = (m // 2) % 2 * 2 + e // nz
    right = (m + 1) % nm
    left = (m + nm - 1) % nm
    partner = m + 1 - 2 * core
    base = m * (2 * REACH)

    def at_y(k):
        return e, (y + k) % ny * 4 + m % 4

    def at_x(k):
        there = (x + k) % 4
        return there % 2 * nz + z, y * 4 + there // 2 * 2 + core

    def at_z(k):
        return e // nz * nz + (z + k) % nz, m

    w_copies = {}
    for layer in range(LAYERS):
        for mat in range(4):
            c = pltpu.make_async_copy(w_hbm.at[layer, mat], w_v.at[layer, mat], w_sem.at[layer, mat])
            c.start()
            w_copies[layer, mat] = c

    barrier = pltpu.get_barrier_semaphore()

    def greet(em, mm):
        pl.semaphore_signal(barrier, inc=1, device_id=(em, mm), device_id_type=MESH)

    greet(e, left)
    greet(e, right)
    for k in range(1, ny):
        greet(*at_y(k))
    for k in range(1, 4):
        greet(*at_x(k))
    for k in range(1, nz):
        greet(*at_z(k))
    pl.semaphore_wait(barrier, 2 + (ny - 1) + 3 + (nz - 1))

    def rcopy(src, dst, ssem, rsem, em, mm):
        c = pltpu.make_async_remote_copy(
            src_ref=src, dst_ref=dst, send_sem=ssem, recv_sem=rsem, device_id=(em, mm), device_id_type=MESH
        )
        c.start()
        return c

    def halo(kind, low, high, dst):
        a = rcopy(high, dst.at[0], hs_sem.at[kind, 0], hr_sem.at[kind, 0], e, right)
        b = rcopy(low, dst.at[1], hs_sem.at[kind, 1], hr_sem.at[kind, 1], e, left)
        return (a, b)

    def wait_recv(pair):
        for c in pair:
            c.wait_recv()

    sent = []
    LOW, HIGH = pl.ds(0, REACH), pl.ds(REACH, REACH)
    h_x1 = halo(0, x_ref.at[0, LOW], x_ref.at[0, HIGH], hx1)

    table = jnp.where(live_ref[...] > 0, nb_ref[...], -100000).astype(F32)
    for half in range(2):
        nl_own[half] = table[:, half * REACH:(half + 1) * REACH]
    h_nl = halo(1, nl_own.at[0], nl_own.at[1], nl_halo)
    stat[...] = jnp.zeros_like(stat)
    cond[...] = jnp.zeros_like(cond)

    emb = emb_ref[...]
    scales, shifts = [], []
    for layer in range(LAYERS):
        pieces = [
            jnp.sum(emb * fw_ref[layer, :, g * 128:(g + 1) * 128], axis=0, keepdims=True) for g in range(8)
        ]
        row = jnp.concatenate(pieces, axis=1)
        scales.append(1.0 + row[:, :D])
        shifts.append(row[:, D:])

    def normalize(states, layer):
        values = states.astype(F32)
        centre = jnp.mean(values, axis=1, keepdims=True)
        off = values - centre
        spread = jnp.mean(off * off, axis=1, keepdims=True)
        inverse = lax.rsqrt(spread + EPSILON)
        u = off * inverse
        return u, inverse, (u * scales[layer] + shifts[layer]).astype(BF16)

    def project_rows(rows, n, layer):
        w = w_v.at[layer]
        qe[layer, rows] = nn(n, w[0]).astype(BF16)
        ke[layer, rows] = nn(n, w[1]).astype(BF16)
        ve[layer, rows] = nn(n, w[2]).astype(BF16)

    def own_rows(src, layer):
        def step(i, carry):
            rows = pl.ds(pl.multiple_of(i * 64, 64), 64)
            u, inverse, n = normalize(src[rows], layer)
            unit[layer, rows] = u
            inv[layer, rows] = jnp.broadcast_to(inverse, (64, 128))
            normed[layer, rows] = n
            return carry

        lax.fori_loop(0, 4, step, 0)
        project_rows(pl.ds(REACH, 2 * REACH), normed[layer], layer)

    def halo_rows(src, layer):
        for side in range(2):
            _, _, n = normalize(src[side], layer)
            project_rows(pl.ds(side * 3 * REACH, REACH), n, layer)

    def attend(layer):
        for b in range(2):
            rows = pl.ds(REACH + b * REACH, REACH)
            window = pl.ds(b * REACH, WIN)
            for h in range(HEADS):
                cols = slice(h * HEAD, (h + 1) * HEAD)
                s = nt(qe[layer, rows, cols], ke[layer, window, cols]) * SCALE2 + bias[b]
                peak = jnp.max(s, axis=1, keepdims=True)
                wts = jnp.exp2(s - peak)
                total = jnp.sum(wts, axis=1, keepdims=True)
                p = wts * (1.0 / total)
                prob[layer, b * HEADS + h] = p
                stat[layer, b * REACH:(b + 1) * REACH, h:h + 1] = peak + jnp.log2(total)
                att[layer, b * REACH:(b + 1) * REACH, cols] = nn(
                    p.astype(BF16), ve[layer, window, cols]
                ).astype(BF16)

    def mask_tile(table, first):
        jid = (lax.broadcasted_iota(jnp.int32, (REACH, REACH), 0) + first).astype(F32)
        out = jnp.full((REACH, REACH), -jnp.inf, F32)
        for s in range(32):
            out = jnp.where(table[s:s + 1, :] == jid, 0.0, out)
        return out

    def own_masks():
        for b in range(2):
            for t in range(3):
                tile = mask_tile(nl_own[b], base + (b + t - 1) * REACH)
                jb = b + t - 1
                if 0 <= jb <= 1:
                    place = b + 1 - jb
                    bias_t[jb, :, place * REACH:(place + 1) * REACH] = tile
                bias[b, :, t * REACH:(t + 1) * REACH] = tile.T

    def halo_masks():
        bias_t[0, :, 0:REACH] = mask_tile(nl_halo[0], base)
        bias_t[1, :, 2 * REACH:] = mask_tile(nl_halo[1], base + REACH)

    for mat in range(3):
        w_copies[0, mat].wait()
    own_rows(x_ref.at[0], 0)
    own_masks()
    wait_recv(h_x1)
    h_cot = halo(2, cot_ref.at[0, LOW], cot_ref.at[0, HIGH], hcot)
    halo_rows(hx1, 0)
    attend(0)
    w_copies[0, 3].wait()
    x2[...] = (x_ref[0].astype(F32) + nn(att[0], w_v[0, 3])).astype(BF16)
    h_x2 = halo(3, x2.at[LOW], x2.at[HIGH], hx2)
    for mat in range(4):
        w_copies[1, mat].wait()
    own_rows(x2, 1)

    wait_recv(h_nl)
    halo_masks()

    def grad_attended(up_own, up_halo, layer, which):
        w3 = w_v[layer, 3]
        if which != 1:
            gae[pl.ds(REACH, 2 * REACH)] = nt(up_own, w3).astype(BF16)
        if which != 0:
            for side in range(2):
                gae[pl.ds(side * 3 * REACH, REACH)] = nt(up_halo[side], w3).astype(BF16)

    wait_recv(h_cot)
    grad_attended(cot_ref[0], hcot, 1, 2)
    wait_recv(h_x2)
    halo_rows(hx2, 1)
    attend(1)

    def query_pass(layer):
        for b in range(2):
            rows = pl.ds(REACH + b * REACH, REACH)
            window = pl.ds(b * REACH, WIN)
            for h in range(HEADS):
                cols = slice(h * HEAD, (h + 1) * HEAD)
                gp = nt(gae[rows, cols], ve[layer, window, cols])
                p = prob[layer, b * HEADS + h]
                delta = jnp.sum(p * gp, axis=1, keepdims=True)
                stat[layer, b * REACH:(b + 1) * REACH, HEADS + h:HEADS + h + 1] = delta
                gs = (p * ((gp - delta) * SCALE)).astype(BF16)
                dq[b * REACH:(b + 1) * REACH, cols] = nn(gs, ke[layer, window, cols]).astype(BF16)
        for half in range(2):
            stat_own[layer, half] = stat[layer, half * REACH:(half + 1) * REACH, :].T[0:8]
        return halo(5 + layer, stat_own.at[layer, 0], stat_own.at[layer, 1], stat_halo.at[layer])

    def key_pass(layer):
        for jb in range(2):
            rows = pl.ds(REACH + jb * REACH, REACH)
            window = pl.ds(jb * REACH, WIN)
            if jb == 0:
                parts = [stat_halo[layer, 0], stat_own[layer, 0], stat_own[layer, 1]]
            else:
                parts = [stat_own[layer, 0], stat_own[layer, 1], stat_halo[layer, 1]]
            stats = jnp.concatenate(parts, axis=1)
            for h in range(HEADS):
                cols = slice(h * HEAD, (h + 1) * HEAD)
                queries = qe[layer, window, cols]
                grads = gae[window, cols]
                s = nt(ke[layer, rows, cols], queries) * SCALE2 + bias_t[jb]
                p = jnp.exp2(s - stats[h:h + 1])
                gp = nt(ve[layer, rows, cols], grads)
                gs = (p * ((gp - stats[HEADS + h:HEADS + h + 1]) * SCALE)).astype(BF16)
                dk[jb * REACH:(jb + 1) * REACH, cols] = nn(gs, queries).astype(BF16)
                dv[jb * REACH:(jb + 1) * REACH, cols] = nn(p.astype(BF16), grads).astype(BF16)

    def order(batch):
        return ((ny, y, at_y), (4, x, at_x)) if batch % 2 == 0 else ((4, x, at_x), (ny, y, at_y))

    def weight_grad(batch, left_side, right_side):
        res = nn(left_side[...].T, right_side[...]).astype(BF16)
        for i in range(nm):
            for xl in range(2):
                py, px = i // 4, i // 2 % 2 * 2 + xl
                place = py * 4 + px if batch % 2 == 0 else px * ny + py
                wb[batch, i % 2, place] = res[i * cw:(i + 1) * cw, xl * 256:(xl + 1) * 256]
        return rcopy(wb.at[batch, 1 - core], rc.at[batch], cs_sem.at[batch], cr_sem.at[batch], e, partner)

    def core_sum(batch, copy):
        copy.wait_recv()
        (n1, c1, at1), (n2, _, _) = order(batch)
        copies = []
        for k in list(range(1, n1)) + [0]:
            block = pl.ds((c1 + k) % n1 * n2, n2)
            s2[batch, block] = (wb[batch, core, block].astype(F32) + rc[batch, block].astype(F32)).astype(BF16)
            if k > 0:
                copies.append(
                    rcopy(
                        s2.at[batch, block], r2.at[batch, k, pl.ds(0, n2)],
                        s2_sem.at[batch, k], r2_sem.at[batch, k], *at1(k),
                    )
                )
        return copies

    def first_sum(batch, copies):
        (n1, c1, _), (n2, c2, at2) = order(batch)
        for c in copies:
            c.wait_recv()
        total = s2[batch, pl.ds(c1 * n2, n2)].astype(F32)
        for k in range(1, n1):
            total = total + r2[batch, k, 0:n2].astype(F32)
        t2[batch, 0:n2] = total.astype(BF16)
        return [
            rcopy(
                t2.at[batch, (c2 + k) % n2], rt.at[batch, k], t2_sem.at[batch, k], rt_sem.at[batch, k], *at2(k)
            )
            for k in range(1, n2)
        ]

    def second_sum(batch, copies):
        _, (n2, c2, _) = order(batch)
        for c in copies:
            c.wait_recv()
        total = t2[batch, c2].astype(F32)
        for k in range(1, n2):
            total = total + rt[batch, k].astype(F32)
        first = (batch % 4) * cw
        acc[batch // 4, first:first + cw] = total

    def start_z(slot):
        whole = acc[slot].T.astype(BF16)
        for i in range(nz):
            s3[slot, i] = whole[i * rw:(i + 1) * rw]
        return [
            rcopy(s3.at[slot, (z + k) % nz], r3.at[slot, k], s3_sem.at[slot, k], r3_sem.at[slot, k], *at_z(k))
            for k in range(1, nz)
        ]

    def z_sum(slot, copies, layer):
        for c in copies:
            c.wait_recv()
        total = s3[slot, z].astype(F32)
        for k in range(1, nz):
            total = total + r3[slot, k].astype(F32)
        for pos, mat in enumerate((3, 0, 1, 2)):
            gw_ref[layer, mat] = total[:, pos * cw:(pos + 1) * cw]

    def input_rows(layer, up, out, i):
        w = w_v.at[layer]
        rows = pl.ds(i * REACH, REACH)
        gn = nt(dq[rows], w[0]) + nt(dk[rows], w[1]) + nt(dv[rows], w[2])
        u = unit[layer, rows]
        gu = gn * u
        first = jnp.sum(gu, axis=0, keepdims=True)
        second = jnp.sum(gn, axis=0, keepdims=True)
        mean_g = jnp.mean(gn * scales[layer], axis=1, keepdims=True)
        mean_gu = jnp.mean(gu * scales[layer], axis=1, keepdims=True)
        centred = gn * scales[layer] - mean_g - u * mean_gu
        out[rows] = (up[rows].astype(F32) + inv[layer, rows][:, 0:1] * centred).astype(BF16)
        return jnp.concatenate([first, second], axis=1)

    def put_cond(layer, row):
        width = 2 * D // nq
        for i in range(nq):
            cond[i, layer:layer + 1] = row[:, i * width:(i + 1) * width]

    core_of, ring_of, turn_of = {}, {}, {}
    core_of[0] = weight_grad(0, cot_ref.at[0], att.at[1])
    st = query_pass(1)
    sent.extend(st)
    core_of[1] = weight_grad(1, dq, normed.at[1])
    ring_of[0] = core_sum(0, core_of[0])
    wait_recv(st)
    key_pass(1)
    row = input_rows(1, cot_ref.at[0], up1, 0)
    up_a = rcopy(up1.at[LOW], hup.at[1], hs_sem.at[4, 1], hr_sem.at[4, 1], e, left)
    row = row + input_rows(1, cot_ref.at[0], up1, 1)
    up_b = rcopy(up1.at[HIGH], hup.at[0], hs_sem.at[4, 0], hr_sem.at[4, 0], e, right)
    put_cond(1, row)
    core_of[2] = weight_grad(2, dk, normed.at[1])
    core_of[3] = weight_grad(3, dv, normed.at[1])
    ring_of[1] = core_sum(1, core_of[1])
    core_of[4] = weight_grad(4, up1, att.at[0])
    grad_attended(up1[...], hup, 0, 0)

    st = query_pass(0)
    sent.extend(st)
    core_of[5] = weight_grad(5, dq, normed.at[0])
    ring_of[2] = core_sum(2, core_of[2])
    ring_of[3] = core_sum(3, core_of[3])
    turn_of[0] = first_sum(0, ring_of[0])
    ring_of[4] = core_sum(4, core_of[4])
    wait_recv((up_a, up_b))
    grad_attended(up1, hup, 0, 1)
    wait_recv(st)
    key_pass(0)
    core_of[6] = weight_grad(6, dk, normed.at[0])
    core_of[7] = weight_grad(7, dv, normed.at[0])
    ring_of[5] = core_sum(5, core_of[5])
    turn_of[1] = first_sum(1, ring_of[1])
    row = input_rows(0, up1, gin_ref.at[0], 0)
    ring_of[6] = core_sum(6, core_of[6])
    ring_of[7] = core_sum(7, core_of[7])
    row = row + input_rows(0, up1, gin_ref.at[0], 1)
    put_cond(0, row)
    core_f = rcopy(cond, rcond, cs_sem.at[8], cr_sem.at[8], e, partner)
    for i in (2, 3, 4, 5):
        turn_of[i] = first_sum(i, ring_of[i])

    core_f.wait_recv()
    s2f[...] = cond[...] + rcond[...]
    y_f = [
        rcopy(s2f.at[pl.ds((y + k) % ny * 2, 2)], ryf.at[k], s3_sem.at[2, k], r3_sem.at[2, k], *at_y(k))
        for k in range(1, ny)
    ]
    for i in range(4):
        second_sum(i, turn_of[i])
    z_b = start_z(0)
    for c in y_f:
        c.wait_recv()
    total = s2f[pl.ds(y * 2, 2)]
    for k in range(1, ny):
        total = total + ryf[k]
    sxf[...] = total
    eye = lax.broadcasted_iota(jnp.int32, (32, 128), 0) == lax.broadcasted_iota(jnp.int32, (32, 128), 1)
    emb_row = jnp.sum(jnp.where(eye, emb, 0.0), axis=0, keepdims=True)
    for half in range(2):
        sxf[half, 2:3, 0:128] = emb_row
    x_f = [
        rcopy(sxf.at[(x + k) % 4 // 2], rxf.at[k], s3_sem.at[3, k], r3_sem.at[3, k], *at_x(k)) for k in range(1, 4)
    ]
    for i in (6, 7):
        turn_of[i] = first_sum(i, ring_of[i])
    for c in x_f:
        c.wait_recv()
    own = sxf[x // 2]
    first_row = lax.broadcasted_iota(jnp.int32, own.shape, 0) < 2
    s3f[0] = own + jnp.where(first_row, rxf[2], 0.0)
    s3f[1] = rxf[1] + jnp.where(first_row, rxf[3], 0.0)
    z_f = [rcopy(s3f, r3f.at[k], s3_sem.at[4, k], r3_sem.at[4, k], *at_z(k)) for k in range(1, nz)]
    for i in range(4, 8):
        second_sum(i, turn_of[i])
    z_a = start_z(1)

    for c in z_f:
        c.wait_recv()
    films = [None] * LAYERS
    for k in range(nz):
        for member in range(2):
            tile = s3f[member] if k == 0 else r3f[k, member]
            column = jnp.sum(jnp.where(eye, tile[2:3, 0:128], 0.0), axis=1, keepdims=True)
            for layer in range(LAYERS):
                part = column * tile[layer:layer + 1]
                films[layer] = part if films[layer] is None else films[layer] + part
    half = 2 * D // nm
    for layer in range(LAYERS):
        gf_ref[layer] = jnp.where(core == 0, films[layer][:, :half], films[layer][:, half:])
    z_sum(0, z_b, 1)
    z_sum(1, z_a, 0)

    for pair in (h_x1, h_nl, h_cot, h_x2, (up_a, up_b)):
        sent.extend(pair)
    sent.extend([core_of[i] for i in range(8)] + [core_f])
    for group in [g[i] for g in (ring_of, turn_of) for i in range(8)] + [y_f, x_f, z_f, z_a, z_b]:
        sent.extend(group)
    for c in sent:
        c.wait_send()


def hand_over(a_ref, b_ref, c_ref, a_out, b_out, c_out):
    a_out[...] = a_ref[...]
    b_out[...] = b_ref[...]
    c_out[...] = c_ref[...]


def body(ne, nm, inputs, cotangent, noise_level, neighbours, live_slots, projections, film_weights):
    emb = noise_features(noise_level)[0]
    emb = jnp.broadcast_to(emb[:, None], (2 * NOISE_FREQ, 128))
    nq, cw, rw, fl = nm // 2, D // nm, D // ne, 4 * D // nm
    ny, nz = nm // 4, ne // 2
    own = 2 * REACH
    vm = pl.BlockSpec(memory_space=pltpu.VMEM)
    V = pltpu.VMEM
    scratch = [
        V((LAYERS, 4, D, D), BF16),
        V((2, REACH, D), BF16), V((2, REACH, D), BF16), V((2, REACH, D), BF16), V((2, REACH, D), BF16),
        V((own, D), BF16), V((own, D), BF16),
        V((LAYERS, own, D), BF16), V((LAYERS, own, D), F32), V((LAYERS, own, 128), F32),
        V((LAYERS, 2 * own, D), BF16), V((LAYERS, 2 * own, D), BF16), V((LAYERS, 2 * own, D), BF16),
        V((2 * own, D), BF16),
        V((LAYERS, 2 * HEADS, REACH, WIN), F32), V((LAYERS, own, D), BF16),
        V((2, REACH, WIN), F32), V((2, REACH, WIN), F32),
        V((2, 32, 128), F32), V((2, 32, 128), F32),
        V((LAYERS, own, 128), F32), V((LAYERS, 2, 8, 128), F32), V((LAYERS, 2, 8, 128), F32),
        V((own, D), BF16), V((own, D), BF16), V((own, D), BF16),
        V((8, 2, 4 * ny, cw, 256), BF16), V((8, 4 * ny, cw, 256), BF16),
        V((8, 4 * ny, cw, 256), BF16), V((8, 4, 4, cw, 256), BF16),
        V((8, 4, cw, 256), BF16), V((8, 4, cw, 256), BF16),
        V((2, 4 * cw, 256), F32), V((2, nz, rw, 4 * cw), BF16), V((2, nz, rw, 4 * cw), BF16),
        V((nq, 8, fl), F32), V((nq, 8, fl), F32), V((nq, 8, fl), F32), V((ny, 2, 8, fl), F32),
        V((2, 8, fl), F32), V((4, 8, fl), F32), V((2, 8, fl), F32), V((nz, 2, 8, fl), F32),
        pltpu.SemaphoreType.DMA((LAYERS, 4)),
        pltpu.SemaphoreType.DMA((7, 2)), pltpu.SemaphoreType.DMA((7, 2)),
        pltpu.SemaphoreType.DMA((9,)), pltpu.SemaphoreType.DMA((9,)),
        pltpu.SemaphoreType.DMA((8, 4)), pltpu.SemaphoreType.DMA((8, 4)),
        pltpu.SemaphoreType.DMA((8, 4)), pltpu.SemaphoreType.DMA((8, 4)),
        pltpu.SemaphoreType.DMA((5, 8)), pltpu.SemaphoreType.DMA((5, 8)),
    ]
    outs = pl.pallas_call(
        functools.partial(kernel, ne, nm),
        out_shape=(
            jax.ShapeDtypeStruct((1, own, D), BF16),
            jax.ShapeDtypeStruct((LAYERS, 4, rw, cw), F32),
            jax.ShapeDtypeStruct((LAYERS, 2 * NOISE_FREQ, fl // 2), F32),
        ),
        in_specs=[vm, vm, vm, vm, vm, pl.BlockSpec(memory_space=pl.ANY), vm],
        out_specs=(vm, vm, vm),
        scratch_shapes=scratch,
        compiler_params=pltpu.CompilerParams(
            collective_id=0, has_side_effects=True, vmem_limit_bytes=56 * 1024 * 1024
        ),
    )(inputs, cotangent, emb, neighbours.T, live_slots.T, projections, film_weights)
    return pl.pallas_call(
        hand_over,
        out_shape=tuple(jax.ShapeDtypeStruct(o.shape, o.dtype) for o in outs),
        in_specs=[vm, vm, vm],
        out_specs=(vm, vm, vm),
    )(*outs)


def solution(mesh):
    placed = (
        P("ens", "mesh", None),
        P("ens", "mesh", None),
        P("ens"),
        P("mesh", None),
        P("mesh", None),
        P(),
        P(),
    )
    return jax.shard_map(
        functools.partial(body, mesh.shape["ens"], mesh.shape["mesh"]),
        mesh=mesh,
        in_specs=placed,
        out_specs=(P("ens", "mesh", None), P(None, None, "ens", "mesh"), P(None, None, "mesh")),
        check_vma=False,
    )
```

```python
import functools
import math

import jax
import jax.numpy as jnp
from jax import lax
from jax.experimental import pallas as pl
from jax.experimental.pallas import tpu as pltpu
from jax.sharding import PartitionSpec as P

HEADS = 4
NOISE_FREQ = 16
LAYERS = 2
EPSILON = 1e-05
MESH = pl.DeviceIdType.MESH
F32 = jnp.float32
BF16 = jnp.bfloat16
REACH = 128
WIN = 3 * REACH
CHUNK = 32
D = 512
HEAD = D // HEADS
SCALE = 1.0 / math.sqrt(HEAD)
SCALE2 = SCALE * math.log2(math.e)


def noise_features(noise_level):
    frequency = jnp.arange(1, NOISE_FREQ + 1).astype(jnp.float32)
    angles = jnp.log(noise_level)[:, None] * frequency[None, :]
    return jnp.concatenate([jnp.sin(angles), jnp.cos(angles)], axis=1)


def nn(a, b):
    return lax.dot_general(a, b, (((1,), (0,)), ((), ())), preferred_element_type=F32)


def nt(a, b):
    return lax.dot_general(a, b, (((1,), (1,)), ((), ())), preferred_element_type=F32)


def kernel(
    ne, nm,
    x_ref, cot_ref, emb_ref, nb_ref, live_ref, w_hbm, fw_ref,
    gin_ref, gw_ref, gf_ref,
    w_v, hx1, hx2, hcot, hup, x2, up1, normed, unit, inv, qe, ke, ve, gae, prob, att,
    bias, bias_t, nl_own, nl_halo, stat, stat_own, stat_halo,
    dq, dk, dv, raw_a, raw_b, half_a, half_b, normed_halo, gn_rows, wb, rc, s2, r2, t2, rt, acc, s3, r3, cond, rcond, s2f, ryf, sxf, rxf, s3f, r3f,
    w_sem, hs_sem, hr_sem, cs_sem, cr_sem, s2_sem, r2_sem, t2_sem, rt_sem, s3_sem, r3_sem,
):
    nq = nm // 2
    cw = D // nm
    rw = D // ne
    e = lax.axis_index("ens")
    m = lax.axis_index("mesh")
    ny, nz = nm // 4, ne // 2
    core = m % 2
    y = m // 4
    z = e % nz
    x = (m // 2) % 2 * 2 + e // nz
    right = (m + 1) % nm
    left = (m + nm - 1) % nm
    partner = m + 1 - 2 * core
    base = m * (2 * REACH)

    def at_y(k):
        return e, (y + k) % ny * 4 + m % 4

    def at_x(k):
        there = (x + k) % 4
        return there % 2 * nz + z, y * 4 + there // 2 * 2 + core

    def at_z(k):
        return e // nz * nz + (z + k) % nz, m

    w_copies = {}
    for layer in range(LAYERS):
        for mat in range(4):
            c = pltpu.make_async_copy(w_hbm.at[layer, mat], w_v.at[layer, mat], w_sem.at[layer, mat])
            c.start()
            w_copies[layer, mat] = c

    barrier = pltpu.get_barrier_semaphore()

    def greet(em, mm):
        pl.semaphore_signal(barrier, inc=1, device_id=(em, mm), device_id_type=MESH)

    greet(e, left)
    greet(e, right)
    for k in range(1, ny):
        greet(*at_y(k))
    for k in range(1, 4):
        greet(*at_x(k))
    for k in range(1, nz):
        greet(*at_z(k))
    pl.semaphore_wait(barrier, 2 + (ny - 1) + 3 + (nz - 1))

    def rcopy(src, dst, ssem, rsem, em, mm):
        c = pltpu.make_async_remote_copy(
            src_ref=src, dst_ref=dst, send_sem=ssem, recv_sem=rsem, device_id=(em, mm), device_id_type=MESH
        )
        c.start()
        return c

    def halo(kind, low, high, dst):
        a = rcopy(high, dst.at[0], hs_sem.at[kind, 0], hr_sem.at[kind, 0], e, right)
        b = rcopy(low, dst.at[1], hs_sem.at[kind, 1], hr_sem.at[kind, 1], e, left)
        return (a, b)

    def wait_recv(pair):
        for c in pair:
            c.wait_recv()

    sent = []
    LOW, HIGH = pl.ds(0, REACH), pl.ds(REACH, REACH)
    h_x1 = halo(0, x_ref.at[0, LOW], x_ref.at[0, HIGH], hx1)

    table = jnp.where(live_ref[...] > 0, nb_ref[...], -100000).astype(F32)
    for half in range(2):
        nl_own[half] = table[:, half * REACH:(half + 1) * REACH]
    h_nl = halo(1, nl_own.at[0], nl_own.at[1], nl_halo)
    stat[...] = jnp.zeros_like(stat)
    cond[...] = jnp.zeros_like(cond)

    emb = emb_ref[...]
    scales, shifts = [], []
    for layer in range(LAYERS):
        pieces = [
            jnp.sum(emb * fw_ref[layer, :, g * 128:(g + 1) * 128], axis=0, keepdims=True) for g in range(8)
        ]
        row = jnp.concatenate(pieces, axis=1)
        scales.append(1.0 + row[:, :D])
        shifts.append(row[:, D:])

    def normalize(states, layer):
        values = states.astype(F32)
        centre = jnp.mean(values, axis=1, keepdims=True)
        off = values - centre
        spread = jnp.mean(off * off, axis=1, keepdims=True)
        inverse = lax.rsqrt(spread + EPSILON)
        u = off * inverse
        return u, inverse, (u * scales[layer] + shifts[layer]).astype(BF16)

    def project_rows(rows, n, layer):
        w = w_v.at[layer]
        qe[layer, rows] = nn(n, w[0]).astype(BF16)
        ke[layer, rows] = nn(n, w[1]).astype(BF16)
        ve[layer, rows] = nn(n, w[2]).astype(BF16)

    def own_rows(src, layer):
        for i in range(2 * REACH // CHUNK):
            rows = pl.ds(i * CHUNK, CHUNK)
            u, inverse, n = normalize(src[rows], layer)
            unit[layer, rows] = u
            inv[layer, rows] = jnp.broadcast_to(inverse, (CHUNK, 128))
            normed[layer, rows] = n
        project_rows(pl.ds(REACH, 2 * REACH), normed[layer], layer)

    def halo_rows(src, layer):
        for side in range(2):
            for i in range(REACH // CHUNK):
                rows = pl.ds(i * CHUNK, CHUNK)
                _, _, n = normalize(src[side, rows], layer)
                normed_halo[side, rows] = n
            project_rows(pl.ds(side * 3 * REACH, REACH), normed_halo[side], layer)

    BLOCKS = [(b, h) for b in range(2) for h in range(HEADS)]

    def spans(b, h):
        return (
            pl.ds(REACH + b * REACH, REACH),
            pl.ds(b * REACH, WIN),
            slice(h * HEAD, (h + 1) * HEAD),
            slice(b * REACH, (b + 1) * REACH),
        )

    def by_rows(step):
        for b, h in BLOCKS:
            for i in range(REACH // CHUNK):
                step(b, h, pl.ds(i * CHUNK, CHUNK))

    def attend(layer):
        for b, h in BLOCKS:
            rows, window, cols, _ = spans(b, h)
            raw_a[b * HEADS + h] = nt(qe[layer, rows, cols], ke[layer, window, cols])

        def soften(b, h, rows):
            s = raw_a[b * HEADS + h, rows] * SCALE2 + bias[b, rows]
            peak = jnp.max(s, axis=1, keepdims=True)
            wts = jnp.exp2(s - peak)
            total = jnp.sum(wts, axis=1, keepdims=True)
            p = wts * (1.0 / total)
            prob[layer, b * HEADS + h, rows] = p
            half_a[b * HEADS + h, rows] = p.astype(BF16)
            stat[layer, pl.ds(b * REACH + rows.start, CHUNK), h:h + 1] = peak + jnp.log2(total)

        by_rows(soften)
        for b, h in BLOCKS:
            _, window, cols, own = spans(b, h)
            att[layer, own, cols] = nn(half_a[b * HEADS + h], ve[layer, window, cols]).astype(BF16)

    def mask_tile(table, first):
        jid = (lax.broadcasted_iota(jnp.int32, (REACH, REACH), 0) + first).astype(F32)
        out = jnp.full((REACH, REACH), -jnp.inf, F32)
        for s in range(32):
            out = jnp.where(table[s:s + 1, :] == jid, 0.0, out)
        return out

    def own_masks():
        for b in range(2):
            for t in range(3):
                tile = mask_tile(nl_own[b], base + (b + t - 1) * REACH)
                jb = b + t - 1
                if 0 <= jb <= 1:
                    place = b + 1 - jb
                    bias_t[jb, :, place * REACH:(place + 1) * REACH] = tile
                bias[b, :, t * REACH:(t + 1) * REACH] = tile.T

    def halo_masks():
        bias_t[0, :, 0:REACH] = mask_tile(nl_halo[0], base)
        bias_t[1, :, 2 * REACH:] = mask_tile(nl_halo[1], base + REACH)

    for mat in range(3):
        w_copies[0, mat].wait()
    own_rows(x_ref.at[0], 0)
    own_masks()
    wait_recv(h_x1)
    h_cot = halo(2, cot_ref.at[0, LOW], cot_ref.at[0, HIGH], hcot)
    halo_rows(hx1, 0)
    attend(0)
    w_copies[0, 3].wait()
    x2[...] = (x_ref[0].astype(F32) + nn(att[0], w_v[0, 3])).astype(BF16)
    h_x2 = halo(3, x2.at[LOW], x2.at[HIGH], hx2)
    for mat in range(4):
        w_copies[1, mat].wait()
    own_rows(x2, 1)

    wait_recv(h_nl)
    halo_masks()

    def grad_attended(up_own, up_halo, layer, which):
        w3 = w_v[layer, 3]
        if which != 1:
            gae[pl.ds(REACH, 2 * REACH)] = nt(up_own, w3).astype(BF16)
        if which != 0:
            for side in range(2):
                gae[pl.ds(side * 3 * REACH, REACH)] = nt(up_halo[side], w3).astype(BF16)

    wait_recv(h_cot)
    grad_attended(cot_ref[0], hcot, 1, 2)
    wait_recv(h_x2)
    halo_rows(hx2, 1)
    attend(1)

    def query_pass(layer):
        for b, h in BLOCKS:
            rows, window, cols, _ = spans(b, h)
            raw_a[b * HEADS + h] = nt(gae[rows, cols], ve[layer, window, cols])

        def differ(b, h, rows):
            gp = raw_a[b * HEADS + h, rows]
            p = prob[layer, b * HEADS + h, rows]
            delta = jnp.sum(p * gp, axis=1, keepdims=True)
            stat[layer, pl.ds(b * REACH + rows.start, CHUNK), HEADS + h:HEADS + h + 1] = delta
            half_a[b * HEADS + h, rows] = (p * ((gp - delta) * SCALE)).astype(BF16)

        by_rows(differ)
        for b, h in BLOCKS:
            _, window, cols, own = spans(b, h)
            dq[own, cols] = nn(half_a[b * HEADS + h], ke[layer, window, cols]).astype(BF16)
        for half in range(2):
            stat_own[layer, half] = stat[layer, half * REACH:(half + 1) * REACH, :].T[0:8]
        return halo(5 + layer, stat_own.at[layer, 0], stat_own.at[layer, 1], stat_halo.at[layer])

    def key_pass(layer):
        for jb, h in BLOCKS:
            rows, window, cols, _ = spans(jb, h)
            raw_a[jb * HEADS + h] = nt(ke[layer, rows, cols], qe[layer, window, cols])
            raw_b[jb * HEADS + h] = nt(ve[layer, rows, cols], gae[window, cols])
        stats = (
            jnp.concatenate([stat_halo[layer, 0], stat_own[layer, 0], stat_own[layer, 1]], axis=1),
            jnp.concatenate([stat_own[layer, 0], stat_own[layer, 1], stat_halo[layer, 1]], axis=1),
        )

        def differ(jb, h, rows):
            s = raw_a[jb * HEADS + h, rows] * SCALE2 + bias_t[jb, rows]
            p = jnp.exp2(s - stats[jb][h:h + 1])
            gp = raw_b[jb * HEADS + h, rows]
            half_a[jb * HEADS + h, rows] = (p * ((gp - stats[jb][HEADS + h:HEADS + h + 1]) * SCALE)).astype(BF16)
            half_b[jb * HEADS + h, rows] = p.astype(BF16)

        by_rows(differ)
        for jb, h in BLOCKS:
            _, window, cols, own = spans(jb, h)
            dk[own, cols] = nn(half_a[jb * HEADS + h], qe[layer, window, cols]).astype(BF16)
            dv[own, cols] = nn(half_b[jb * HEADS + h], gae[window, cols]).astype(BF16)

    def order(batch):
        return ((ny, y, at_y), (4, x, at_x)) if batch % 2 == 0 else ((4, x, at_x), (ny, y, at_y))

    def weight_grad(batch, left_side, right_side):
        res = nn(left_side[...].T, right_side[...]).astype(BF16)
        for i in range(nm):
            for xl in range(2):
                py, px = i // 4, i // 2 % 2 * 2 + xl
                place = py * 4 + px if batch % 2 == 0 else px * ny + py
                wb[batch, i % 2, place] = res[i * cw:(i + 1) * cw, xl * 256:(xl + 1) * 256]
        return rcopy(wb.at[batch, 1 - core], rc.at[batch], cs_sem.at[batch], cr_sem.at[batch], e, partner)

    def core_sum(batch, copy):
        copy.wait_recv()
        (n1, c1, at1), (n2, _, _) = order(batch)
        copies = []
        for k in list(range(1, n1)) + [0]:
            block = pl.ds((c1 + k) % n1 * n2, n2)
            s2[batch, block] = (wb[batch, core, block].astype(F32) + rc[batch, block].astype(F32)).astype(BF16)
            if k > 0:
                copies.append(
                    rcopy(
                        s2.at[batch, block], r2.at[batch, k, pl.ds(0, n2)],
                        s2_sem.at[batch, k], r2_sem.at[batch, k], *at1(k),
                    )
                )
        return copies

    def first_sum(batch, copies):
        (n1, c1, _), (n2, c2, at2) = order(batch)
        for c in copies:
            c.wait_recv()
        total = s2[batch, pl.ds(c1 * n2, n2)].astype(F32)
        for k in range(1, n1):
            total = total + r2[batch, k, 0:n2].astype(F32)
        t2[batch, 0:n2] = total.astype(BF16)
        return [
            rcopy(
                t2.at[batch, (c2 + k) % n2], rt.at[batch, k], t2_sem.at[batch, k], rt_sem.at[batch, k], *at2(k)
            )
            for k in range(1, n2)
        ]

    def second_sum(batch, copies):
        _, (n2, c2, _) = order(batch)
        for c in copies:
            c.wait_recv()
        total = t2[batch, c2].astype(F32)
        for k in range(1, n2):
            total = total + rt[batch, k].astype(F32)
        first = (batch % 4) * cw
        acc[batch // 4, first:first + cw] = total

    def start_z(slot):
        whole = acc[slot].T.astype(BF16)
        for i in range(nz):
            s3[slot, i] = whole[i * rw:(i + 1) * rw]
        return [
            rcopy(s3.at[slot, (z + k) % nz], r3.at[slot, k], s3_sem.at[slot, k], r3_sem.at[slot, k], *at_z(k))
            for k in range(1, nz)
        ]

    def z_sum(slot, copies, layer):
        for c in copies:
            c.wait_recv()
        total = s3[slot, z].astype(F32)
        for k in range(1, nz):
            total = total + r3[slot, k].astype(F32)
        for pos, mat in enumerate((3, 0, 1, 2)):
            gw_ref[layer, mat] = total[:, pos * cw:(pos + 1) * cw]

    def input_rows(layer, up, out, i):
        w = w_v.at[layer]
        block = pl.ds(i * REACH, REACH)
        gn_rows[...] = nt(dq[block], w[0]) + nt(dk[block], w[1]) + nt(dv[block], w[2])
        first, second = jnp.zeros((1, D), F32), jnp.zeros((1, D), F32)
        for j in range(REACH // CHUNK):
            rows = pl.ds(i * REACH + j * CHUNK, CHUNK)
            gn = gn_rows[pl.ds(j * CHUNK, CHUNK)]
            u = unit[layer, rows]
            gu = gn * u
            first = first + jnp.sum(gu, axis=0, keepdims=True)
            second = second + jnp.sum(gn, axis=0, keepdims=True)
            g = gn * scales[layer]
            mean_g = jnp.mean(g, axis=1, keepdims=True)
            mean_gu = jnp.mean(gu * scales[layer], axis=1, keepdims=True)
            centred = g - mean_g - u * mean_gu
            out[rows] = (up[rows].astype(F32) + inv[layer, rows][:, 0:1] * centred).astype(BF16)
        return jnp.concatenate([first, second], axis=1)

    def put_cond(layer, row):
        width = 2 * D // nq
        for i in range(nq):
            cond[i, layer:layer + 1] = row[:, i * width:(i + 1) * width]

    core_of, ring_of, turn_of = {}, {}, {}
    core_of[0] = weight_grad(0, cot_ref.at[0], att.at[1])
    st = query_pass(1)
    sent.extend(st)
    core_of[1] = weight_grad(1, dq, normed.at[1])
    ring_of[0] = core_sum(0, core_of[0])
    wait_recv(st)
    key_pass(1)
    row = input_rows(1, cot_ref.at[0], up1, 0)
    up_a = rcopy(up1.at[LOW], hup.at[1], hs_sem.at[4, 1], hr_sem.at[4, 1], e, left)
    row = row + input_rows(1, cot_ref.at[0], up1, 1)
    up_b = rcopy(up1.at[HIGH], hup.at[0], hs_sem.at[4, 0], hr_sem.at[4, 0], e, right)
    put_cond(1, row)
    core_of[2] = weight_grad(2, dk, normed.at[1])
    core_of[3] = weight_grad(3, dv, normed.at[1])
    ring_of[1] = core_sum(1, core_of[1])
    core_of[4] = weight_grad(4, up1, att.at[0])
    grad_attended(up1[...], hup, 0, 0)

    st = query_pass(0)
    sent.extend(st)
    core_of[5] = weight_grad(5, dq, normed.at[0])
    ring_of[2] = core_sum(2, core_of[2])
    ring_of[3] = core_sum(3, core_of[3])
    turn_of[0] = first_sum(0, ring_of[0])
    ring_of[4] = core_sum(4, core_of[4])
    wait_recv((up_a, up_b))
    grad_attended(up1, hup, 0, 1)
    ring_of[5] = core_sum(5, core_of[5])
    turn_of[1] = first_sum(1, ring_of[1])
    wait_recv(st)
    key_pass(0)
    core_of[6] = weight_grad(6, dk, normed.at[0])
    core_of[7] = weight_grad(7, dv, normed.at[0])
    row = input_rows(0, up1, gin_ref.at[0], 0)
    ring_of[6] = core_sum(6, core_of[6])
    ring_of[7] = core_sum(7, core_of[7])
    row = row + input_rows(0, up1, gin_ref.at[0], 1)
    put_cond(0, row)
    core_f = rcopy(cond, rcond, cs_sem.at[8], cr_sem.at[8], e, partner)
    for i in (2, 3, 4, 5):
        turn_of[i] = first_sum(i, ring_of[i])

    core_f.wait_recv()
    s2f[...] = cond[...] + rcond[...]
    y_f = [
        rcopy(s2f.at[pl.ds((y + k) % ny * 2, 2)], ryf.at[k], s3_sem.at[2, k], r3_sem.at[2, k], *at_y(k))
        for k in range(1, ny)
    ]
    for i in range(4):
        second_sum(i, turn_of[i])
    z_b = start_z(0)
    for c in y_f:
        c.wait_recv()
    total = s2f[pl.ds(y * 2, 2)]
    for k in range(1, ny):
        total = total + ryf[k]
    sxf[...] = total
    eye = lax.broadcasted_iota(jnp.int32, (32, 128), 0) == lax.broadcasted_iota(jnp.int32, (32, 128), 1)
    emb_row = jnp.sum(jnp.where(eye, emb, 0.0), axis=0, keepdims=True)
    for half in range(2):
        sxf[half, 2:3, 0:128] = emb_row
    x_f = [
        rcopy(sxf.at[(x + k) % 4 // 2], rxf.at[k], s3_sem.at[3, k], r3_sem.at[3, k], *at_x(k)) for k in range(1, 4)
    ]
    for i in (6, 7):
        turn_of[i] = first_sum(i, ring_of[i])
    for c in x_f:
        c.wait_recv()
    own = sxf[x // 2]
    first_row = lax.broadcasted_iota(jnp.int32, own.shape, 0) < 2
    s3f[0] = own + jnp.where(first_row, rxf[2], 0.0)
    s3f[1] = rxf[1] + jnp.where(first_row, rxf[3], 0.0)
    z_f = [rcopy(s3f, r3f.at[k], s3_sem.at[4, k], r3_sem.at[4, k], *at_z(k)) for k in range(1, nz)]
    for i in range(4, 8):
        second_sum(i, turn_of[i])
    z_a = start_z(1)

    for c in z_f:
        c.wait_recv()
    films = [None] * LAYERS
    for k in range(nz):
        for member in range(2):
            tile = s3f[member] if k == 0 else r3f[k, member]
            column = jnp.sum(jnp.where(eye, tile[2:3, 0:128], 0.0), axis=1, keepdims=True)
            for layer in range(LAYERS):
                part = column * tile[layer:layer + 1]
                films[layer] = part if films[layer] is None else films[layer] + part
    half = 2 * D // nm
    for layer in range(LAYERS):
        gf_ref[layer] = jnp.where(core == 0, films[layer][:, :half], films[layer][:, half:])
    z_sum(0, z_b, 1)
    z_sum(1, z_a, 0)

    for pair in (h_x1, h_nl, h_cot, h_x2, (up_a, up_b)):
        sent.extend(pair)
    sent.extend([core_of[i] for i in range(8)] + [core_f])
    for group in [g[i] for g in (ring_of, turn_of) for i in range(8)] + [y_f, x_f, z_f, z_a, z_b]:
        sent.extend(group)
    for c in sent:
        c.wait_send()


def hand_over(a_ref, b_ref, c_ref, a_out, b_out, c_out):
    a_out[...] = a_ref[...]
    b_out[...] = b_ref[...]
    c_out[...] = c_ref[...]


def body(ne, nm, inputs, cotangent, noise_level, neighbours, live_slots, projections, film_weights):
    emb = noise_features(noise_level)[0]
    emb = jnp.broadcast_to(emb[:, None], (2 * NOISE_FREQ, 128))
    nq, cw, rw, fl = nm // 2, D // nm, D // ne, 4 * D // nm
    ny, nz = nm // 4, ne // 2
    own = 2 * REACH
    vm = pl.BlockSpec(memory_space=pltpu.VMEM)
    V = pltpu.VMEM
    scratch = [
        V((LAYERS, 4, D, D), BF16),
        V((2, REACH, D), BF16), V((2, REACH, D), BF16), V((2, REACH, D), BF16), V((2, REACH, D), BF16),
        V((own, D), BF16), V((own, D), BF16),
        V((LAYERS, own, D), BF16), V((LAYERS, own, D), F32), V((LAYERS, own, 128), F32),
        V((LAYERS, 2 * own, D), BF16), V((LAYERS, 2 * own, D), BF16), V((LAYERS, 2 * own, D), BF16),
        V((2 * own, D), BF16),
        V((LAYERS, 2 * HEADS, REACH, WIN), F32), V((LAYERS, own, D), BF16),
        V((2, REACH, WIN), F32), V((2, REACH, WIN), F32),
        V((2, 32, 128), F32), V((2, 32, 128), F32),
        V((LAYERS, own, 128), F32), V((LAYERS, 2, 8, 128), F32), V((LAYERS, 2, 8, 128), F32),
        V((own, D), BF16), V((own, D), BF16), V((own, D), BF16),
        V((2 * HEADS, REACH, WIN), F32), V((2 * HEADS, REACH, WIN), F32),
        V((2 * HEADS, REACH, WIN), BF16), V((2 * HEADS, REACH, WIN), BF16),
        V((2, REACH, D), BF16), V((REACH, D), F32),
        V((8, 2, 4 * ny, cw, 256), BF16), V((8, 4 * ny, cw, 256), BF16),
        V((8, 4 * ny, cw, 256), BF16), V((8, 4, 4, cw, 256), BF16),
        V((8, 4, cw, 256), BF16), V((8, 4, cw, 256), BF16),
        V((2, 4 * cw, 256), F32), V((2, nz, rw, 4 * cw), BF16), V((2, nz, rw, 4 * cw), BF16),
        V((nq, 8, fl), F32), V((nq, 8, fl), F32), V((nq, 8, fl), F32), V((ny, 2, 8, fl), F32),
        V((2, 8, fl), F32), V((4, 8, fl), F32), V((2, 8, fl), F32), V((nz, 2, 8, fl), F32),
        pltpu.SemaphoreType.DMA((LAYERS, 4)),
        pltpu.SemaphoreType.DMA((7, 2)), pltpu.SemaphoreType.DMA((7, 2)),
        pltpu.SemaphoreType.DMA((9,)), pltpu.SemaphoreType.DMA((9,)),
        pltpu.SemaphoreType.DMA((8, 4)), pltpu.SemaphoreType.DMA((8, 4)),
        pltpu.SemaphoreType.DMA((8, 4)), pltpu.SemaphoreType.DMA((8, 4)),
        pltpu.SemaphoreType.DMA((5, 8)), pltpu.SemaphoreType.DMA((5, 8)),
    ]
    outs = pl.pallas_call(
        functools.partial(kernel, ne, nm),
        out_shape=(
            jax.ShapeDtypeStruct((1, own, D), BF16),
            jax.ShapeDtypeStruct((LAYERS, 4, rw, cw), F32),
            jax.ShapeDtypeStruct((LAYERS, 2 * NOISE_FREQ, fl // 2), F32),
        ),
        in_specs=[vm, vm, vm, vm, vm, pl.BlockSpec(memory_space=pl.ANY), vm],
        out_specs=(vm, vm, vm),
        scratch_shapes=scratch,
        compiler_params=pltpu.CompilerParams(
            collective_id=0, has_side_effects=True, vmem_limit_bytes=56 * 1024 * 1024
        ),
    )(inputs, cotangent, emb, neighbours.T, live_slots.T, projections, film_weights)
    return pl.pallas_call(
        hand_over,
        out_shape=tuple(jax.ShapeDtypeStruct(o.shape, o.dtype) for o in outs),
        in_specs=[vm, vm, vm],
        out_specs=(vm, vm, vm),
    )(*outs)


def solution(mesh):
    placed = (
        P("ens", "mesh", None),
        P("ens", "mesh", None),
        P("ens"),
        P("mesh", None),
        P("mesh", None),
        P(),
        P(),
    )
    return jax.shard_map(
        functools.partial(body, mesh.shape["ens"], mesh.shape["mesh"]),
        mesh=mesh,
        in_specs=placed,
        out_specs=(P("ens", "mesh", None), P(None, None, "ens", "mesh"), P(None, None, "mesh")),
        check_vma=False,
    )
```

```python
import functools
import math

import jax
import jax.numpy as jnp
from jax import lax
from jax.experimental import pallas as pl
from jax.experimental.pallas import tpu as pltpu
from jax.sharding import PartitionSpec as P

HEADS = 4
NOISE_FREQ = 16
LAYERS = 2
EPSILON = 1e-05
MESH = pl.DeviceIdType.MESH
F32 = jnp.float32
BF16 = jnp.bfloat16
REACH = 128
WIN = 3 * REACH
CHUNK = 32
D = 512
HEAD = D // HEADS
SCALE = 1.0 / math.sqrt(HEAD)
SCALE2 = SCALE * math.log2(math.e)


def noise_features(noise_level):
    frequency = jnp.arange(1, NOISE_FREQ + 1).astype(jnp.float32)
    angles = jnp.log(noise_level)[:, None] * frequency[None, :]
    return jnp.concatenate([jnp.sin(angles), jnp.cos(angles)], axis=1)


def nn(a, b):
    return lax.dot_general(a, b, (((1,), (0,)), ((), ())), preferred_element_type=F32)


def nt(a, b):
    return lax.dot_general(a, b, (((1,), (1,)), ((), ())), preferred_element_type=F32)


def kernel(
    ne, nm,
    x_ref, cot_ref, emb_ref, nb_ref, live_ref, w_hbm, fw_ref,
    gin_ref, gw_ref, gf_ref,
    w_v, hx1, hx2, hcot, hup, x2, up1, normed, unit, inv, qe, ke, ve, gae, prob, att,
    bias, bias_t, nl_own, nl_halo, stat, stat_own, stat_halo,
    dq, dk, dv, raw_a, raw_b, half_a, half_b, normed_halo, gn_rows, wb, rc, s2, r2, t2, rt, acc, s3, r3, cond, rcond, s2f, ryf, sxf, rxf, s3f, r3f,
    w_sem, hs_sem, hr_sem, cs_sem, cr_sem, s2_sem, r2_sem, t2_sem, rt_sem, s3_sem, r3_sem,
):
    nq = nm // 2
    cw = D // nm
    rw = D // ne
    e = lax.axis_index("ens")
    m = lax.axis_index("mesh")
    ny, nz = nm // 4, ne // 2
    core = m % 2
    y = m // 4
    z = e % nz
    x = (m // 2) % 2 * 2 + e // nz
    right = (m + 1) % nm
    left = (m + nm - 1) % nm
    partner = m + 1 - 2 * core
    base = m * (2 * REACH)

    def at_y(k):
        return e, (y + k) % ny * 4 + m % 4

    def at_x(k):
        there = (x + k) % 4
        return there % 2 * nz + z, y * 4 + there // 2 * 2 + core

    def at_z(k):
        return e // nz * nz + (z + k) % nz, m

    w_copies = {}
    for layer in range(LAYERS):
        for mat in range(4):
            c = pltpu.make_async_copy(w_hbm.at[layer, mat], w_v.at[layer, mat], w_sem.at[layer, mat])
            c.start()
            w_copies[layer, mat] = c

    barrier = pltpu.get_barrier_semaphore()

    def greet(em, mm):
        pl.semaphore_signal(barrier, inc=1, device_id=(em, mm), device_id_type=MESH)

    greet(e, left)
    greet(e, right)
    for k in range(1, ny):
        greet(*at_y(k))
    for k in range(1, 4):
        greet(*at_x(k))
    for k in range(1, nz):
        greet(*at_z(k))
    pl.semaphore_wait(barrier, 2 + (ny - 1) + 3 + (nz - 1))

    def rcopy(src, dst, ssem, rsem, em, mm):
        c = pltpu.make_async_remote_copy(
            src_ref=src, dst_ref=dst, send_sem=ssem, recv_sem=rsem, device_id=(em, mm), device_id_type=MESH
        )
        c.start()
        return c

    def halo(kind, low, high, dst):
        a = rcopy(high, dst.at[0], hs_sem.at[kind, 0], hr_sem.at[kind, 0], e, right)
        b = rcopy(low, dst.at[1], hs_sem.at[kind, 1], hr_sem.at[kind, 1], e, left)
        return (a, b)

    def wait_recv(pair):
        for c in pair:
            c.wait_recv()

    sent = []
    LOW, HIGH = pl.ds(0, REACH), pl.ds(REACH, REACH)
    h_x1 = halo(0, x_ref.at[0, LOW], x_ref.at[0, HIGH], hx1)

    table = jnp.where(live_ref[...] > 0, nb_ref[...], -100000).astype(F32)
    for half in range(2):
        nl_own[half] = table[:, half * REACH:(half + 1) * REACH]
    h_nl = halo(1, nl_own.at[0], nl_own.at[1], nl_halo)
    stat[...] = jnp.zeros_like(stat)
    cond[...] = jnp.zeros_like(cond)

    emb = emb_ref[...]
    scales, shifts = [], []
    for layer in range(LAYERS):
        pieces = [
            jnp.sum(emb * fw_ref[layer, :, g * 128:(g + 1) * 128], axis=0, keepdims=True) for g in range(8)
        ]
        row = jnp.concatenate(pieces, axis=1)
        scales.append(1.0 + row[:, :D])
        shifts.append(row[:, D:])

    def normalize(states, layer):
        values = states.astype(F32)
        centre = jnp.mean(values, axis=1, keepdims=True)
        off = values - centre
        spread = jnp.mean(off * off, axis=1, keepdims=True)
        inverse = lax.rsqrt(spread + EPSILON)
        u = off * inverse
        return u, inverse, (u * scales[layer] + shifts[layer]).astype(BF16)

    def project_rows(rows, n, layer):
        w = w_v.at[layer]
        qe[layer, rows] = nn(n, w[0]).astype(BF16)
        ke[layer, rows] = nn(n, w[1]).astype(BF16)
        ve[layer, rows] = nn(n, w[2]).astype(BF16)

    def own_rows(src, layer):
        for i in range(2 * REACH // CHUNK):
            rows = pl.ds(i * CHUNK, CHUNK)
            u, inverse, n = normalize(src[rows], layer)
            unit[layer, rows] = u
            inv[layer, rows] = jnp.broadcast_to(inverse, (CHUNK, 128))
            normed[layer, rows] = n
        project_rows(pl.ds(REACH, 2 * REACH), normed[layer], layer)

    def halo_rows(src, layer):
        for side in range(2):
            for i in range(REACH // CHUNK):
                rows = pl.ds(i * CHUNK, CHUNK)
                _, _, n = normalize(src[side, rows], layer)
                normed_halo[side, rows] = n
            project_rows(pl.ds(side * 3 * REACH, REACH), normed_halo[side], layer)

    BLOCKS = [(b, h) for b in range(2) for h in range(HEADS)]

    def spans(b, h):
        return (
            pl.ds(REACH + b * REACH, REACH),
            pl.ds(b * REACH, WIN),
            slice(h * HEAD, (h + 1) * HEAD),
            slice(b * REACH, (b + 1) * REACH),
        )

    def by_rows(step):
        for b, h in BLOCKS:
            for i in range(REACH // CHUNK):
                step(b, h, pl.ds(i * CHUNK, CHUNK))

    def attend(layer):
        for b, h in BLOCKS:
            rows, window, cols, _ = spans(b, h)
            raw_a[b * HEADS + h] = nt(qe[layer, rows, cols], ke[layer, window, cols])

        def soften(b, h, rows):
            s = raw_a[b * HEADS + h, rows] * SCALE2 + bias[b, rows]
            peak = jnp.max(s, axis=1, keepdims=True)
            wts = jnp.exp2(s - peak)
            total = jnp.sum(wts, axis=1, keepdims=True)
            p = wts * (1.0 / total)
            prob[layer, b * HEADS + h, rows] = p
            half_a[b * HEADS + h, rows] = p.astype(BF16)
            stat[layer, pl.ds(b * REACH + rows.start, CHUNK), h:h + 1] = peak + jnp.log2(total)

        by_rows(soften)
        for b, h in BLOCKS:
            _, window, cols, own = spans(b, h)
            att[layer, own, cols] = nn(half_a[b * HEADS + h], ve[layer, window, cols]).astype(BF16)

    def mask_tile(table, first):
        jid = (lax.broadcasted_iota(jnp.int32, (REACH, REACH), 0) + first).astype(F32)
        out = jnp.full((REACH, REACH), -jnp.inf, F32)
        for s in range(32):
            out = jnp.where(table[s:s + 1, :] == jid, 0.0, out)
        return out

    def own_masks():
        for b in range(2):
            for t in range(3):
                tile = mask_tile(nl_own[b], base + (b + t - 1) * REACH)
                jb = b + t - 1
                if 0 <= jb <= 1:
                    place = b + 1 - jb
                    bias_t[jb, :, place * REACH:(place + 1) * REACH] = tile
                bias[b, :, t * REACH:(t + 1) * REACH] = tile.T

    def halo_masks():
        bias_t[0, :, 0:REACH] = mask_tile(nl_halo[0], base)
        bias_t[1, :, 2 * REACH:] = mask_tile(nl_halo[1], base + REACH)

    for mat in range(3):
        w_copies[0, mat].wait()
    own_rows(x_ref.at[0], 0)
    own_masks()
    wait_recv(h_x1)
    h_cot = halo(2, cot_ref.at[0, LOW], cot_ref.at[0, HIGH], hcot)
    halo_rows(hx1, 0)
    attend(0)
    w_copies[0, 3].wait()
    x2[...] = (x_ref[0].astype(F32) + nn(att[0], w_v[0, 3])).astype(BF16)
    h_x2 = halo(3, x2.at[LOW], x2.at[HIGH], hx2)
    for mat in range(4):
        w_copies[1, mat].wait()
    own_rows(x2, 1)

    wait_recv(h_nl)
    halo_masks()

    def grad_attended(up_own, up_halo, layer, which):
        w3 = w_v[layer, 3]
        if which != 1:
            gae[pl.ds(REACH, 2 * REACH)] = nt(up_own, w3).astype(BF16)
        if which != 0:
            for side in range(2):
                gae[pl.ds(side * 3 * REACH, REACH)] = nt(up_halo[side], w3).astype(BF16)

    wait_recv(h_cot)
    grad_attended(cot_ref[0], hcot, 1, 2)
    wait_recv(h_x2)
    halo_rows(hx2, 1)
    attend(1)

    def query_pass(layer):
        for b, h in BLOCKS:
            rows, window, cols, _ = spans(b, h)
            raw_a[b * HEADS + h] = nt(gae[rows, cols], ve[layer, window, cols])

        def differ(b, h, rows):
            gp = raw_a[b * HEADS + h, rows]
            p = prob[layer, b * HEADS + h, rows]
            delta = jnp.sum(p * gp, axis=1, keepdims=True)
            stat[layer, pl.ds(b * REACH + rows.start, CHUNK), HEADS + h:HEADS + h + 1] = delta
            half_a[b * HEADS + h, rows] = (p * ((gp - delta) * SCALE)).astype(BF16)

        by_rows(differ)
        for b, h in BLOCKS:
            _, window, cols, own = spans(b, h)
            dq[own, cols] = nn(half_a[b * HEADS + h], ke[layer, window, cols]).astype(BF16)
        for half in range(2):
            stat_own[layer, half] = stat[layer, half * REACH:(half + 1) * REACH, :].T[0:8]
        return halo(5 + layer, stat_own.at[layer, 0], stat_own.at[layer, 1], stat_halo.at[layer])

    def key_pass(layer):
        for jb, h in BLOCKS:
            rows, window, cols, _ = spans(jb, h)
            raw_a[jb * HEADS + h] = nt(ke[layer, rows, cols], qe[layer, window, cols])
            raw_b[jb * HEADS + h] = nt(ve[layer, rows, cols], gae[window, cols])
        stats = (
            jnp.concatenate([stat_halo[layer, 0], stat_own[layer, 0], stat_own[layer, 1]], axis=1),
            jnp.concatenate([stat_own[layer, 0], stat_own[layer, 1], stat_halo[layer, 1]], axis=1),
        )

        def differ(jb, h, rows):
            s = raw_a[jb * HEADS + h, rows] * SCALE2 + bias_t[jb, rows]
            p = jnp.exp2(s - stats[jb][h:h + 1])
            gp = raw_b[jb * HEADS + h, rows]
            half_a[jb * HEADS + h, rows] = (p * ((gp - stats[jb][HEADS + h:HEADS + h + 1]) * SCALE)).astype(BF16)
            half_b[jb * HEADS + h, rows] = p.astype(BF16)

        by_rows(differ)
        for jb, h in BLOCKS:
            _, window, cols, own = spans(jb, h)
            dk[own, cols] = nn(half_a[jb * HEADS + h], qe[layer, window, cols]).astype(BF16)
            dv[own, cols] = nn(half_b[jb * HEADS + h], gae[window, cols]).astype(BF16)

    def order(batch):
        return ((ny, y, at_y), (4, x, at_x)) if batch % 2 == 0 else ((4, x, at_x), (ny, y, at_y))

    def weight_grad(batch, left_side, right_side):
        res = nn(left_side[...].T, right_side[...]).astype(BF16)
        for i in range(nm):
            for xl in range(2):
                py, px = i // 4, i // 2 % 2 * 2 + xl
                place = py * 4 + px if batch % 2 == 0 else px * ny + py
                wb[batch, i % 2, place] = res[i * cw:(i + 1) * cw, xl * 256:(xl + 1) * 256]
        return rcopy(wb.at[batch, 1 - core], rc.at[batch], cs_sem.at[batch], cr_sem.at[batch], e, partner)

    def core_sum(batch, copy):
        copy.wait_recv()
        (n1, c1, at1), (n2, _, _) = order(batch)
        copies = []
        for k in list(range(1, n1)) + [0]:
            block = pl.ds((c1 + k) % n1 * n2, n2)
            s2[batch, block] = (wb[batch, core, block].astype(F32) + rc[batch, block].astype(F32)).astype(BF16)
            if k > 0:
                copies.append(
                    rcopy(
                        s2.at[batch, block], r2.at[batch, k, pl.ds(0, n2)],
                        s2_sem.at[batch, k], r2_sem.at[batch, k], *at1(k),
                    )
                )
        return copies

    def first_sum(batch, copies):
        (n1, c1, _), (n2, c2, at2) = order(batch)
        for c in copies:
            c.wait_recv()
        total = s2[batch, pl.ds(c1 * n2, n2)].astype(F32)
        for k in range(1, n1):
            total = total + r2[batch, k, 0:n2].astype(F32)
        t2[batch, 0:n2] = total.astype(BF16)
        return [
            rcopy(
                t2.at[batch, (c2 + k) % n2], rt.at[batch, k], t2_sem.at[batch, k], rt_sem.at[batch, k], *at2(k)
            )
            for k in range(1, n2)
        ]

    def second_sum(batch, copies):
        _, (n2, c2, _) = order(batch)
        for c in copies:
            c.wait_recv()
        total = t2[batch, c2].astype(F32)
        for k in range(1, n2):
            total = total + rt[batch, k].astype(F32)
        first = (batch % 4) * cw
        acc[batch // 4, first:first + cw] = total

    def start_z(slot):
        whole = acc[slot].T.astype(BF16)
        for i in range(nz):
            s3[slot, i] = whole[i * rw:(i + 1) * rw]
        return [
            rcopy(s3.at[slot, (z + k) % nz], r3.at[slot, k], s3_sem.at[slot, k], r3_sem.at[slot, k], *at_z(k))
            for k in range(1, nz)
        ]

    def z_sum(slot, copies, layer):
        for c in copies:
            c.wait_recv()
        total = s3[slot, z].astype(F32)
        for k in range(1, nz):
            total = total + r3[slot, k].astype(F32)
        for pos, mat in enumerate((3, 0, 1, 2)):
            gw_ref[layer, mat] = total[:, pos * cw:(pos + 1) * cw]

    def input_rows(layer, up, out, i):
        w = w_v.at[layer]
        block = pl.ds(i * REACH, REACH)
        gn_rows[...] = nt(dq[block], w[0]) + nt(dk[block], w[1]) + nt(dv[block], w[2])
        first, second = jnp.zeros((1, D), F32), jnp.zeros((1, D), F32)
        for j in range(REACH // CHUNK):
            rows = pl.ds(i * REACH + j * CHUNK, CHUNK)
            gn = gn_rows[pl.ds(j * CHUNK, CHUNK)]
            u = unit[layer, rows]
            gu = gn * u
            first = first + jnp.sum(gu, axis=0, keepdims=True)
            second = second + jnp.sum(gn, axis=0, keepdims=True)
            g = gn * scales[layer]
            mean_g = jnp.mean(g, axis=1, keepdims=True)
            mean_gu = jnp.mean(gu * scales[layer], axis=1, keepdims=True)
            centred = g - mean_g - u * mean_gu
            out[rows] = (up[rows].astype(F32) + inv[layer, rows][:, 0:1] * centred).astype(BF16)
        return jnp.concatenate([first, second], axis=1)

    def put_cond(layer, row):
        width = 2 * D // nq
        for i in range(nq):
            cond[i, layer:layer + 1] = row[:, i * width:(i + 1) * width]

    core_of, ring_of, turn_of = {}, {}, {}
    core_of[0] = weight_grad(0, cot_ref.at[0], att.at[1])
    st = query_pass(1)
    sent.extend(st)
    ring_of[0] = core_sum(0, core_of[0])
    core_of[1] = weight_grad(1, dq, normed.at[1])
    wait_recv(st)
    ring_of[1] = core_sum(1, core_of[1])
    key_pass(1)
    row = input_rows(1, cot_ref.at[0], up1, 0)
    up_a = rcopy(up1.at[LOW], hup.at[1], hs_sem.at[4, 1], hr_sem.at[4, 1], e, left)
    row = row + input_rows(1, cot_ref.at[0], up1, 1)
    up_b = rcopy(up1.at[HIGH], hup.at[0], hs_sem.at[4, 0], hr_sem.at[4, 0], e, right)
    put_cond(1, row)
    core_of[2] = weight_grad(2, dk, normed.at[1])
    core_of[3] = weight_grad(3, dv, normed.at[1])
    core_of[4] = weight_grad(4, up1, att.at[0])
    grad_attended(up1[...], hup, 0, 0)

    st = query_pass(0)
    sent.extend(st)
    core_of[5] = weight_grad(5, dq, normed.at[0])
    ring_of[2] = core_sum(2, core_of[2])
    ring_of[3] = core_sum(3, core_of[3])
    turn_of[0] = first_sum(0, ring_of[0])
    ring_of[4] = core_sum(4, core_of[4])
    wait_recv((up_a, up_b))
    grad_attended(up1, hup, 0, 1)
    ring_of[5] = core_sum(5, core_of[5])
    turn_of[1] = first_sum(1, ring_of[1])
    wait_recv(st)
    key_pass(0)
    core_of[6] = weight_grad(6, dk, normed.at[0])
    core_of[7] = weight_grad(7, dv, normed.at[0])
    row = input_rows(0, up1, gin_ref.at[0], 0)
    ring_of[6] = core_sum(6, core_of[6])
    ring_of[7] = core_sum(7, core_of[7])
    row = row + input_rows(0, up1, gin_ref.at[0], 1)
    put_cond(0, row)
    core_f = rcopy(cond, rcond, cs_sem.at[8], cr_sem.at[8], e, partner)
    for i in (2, 3, 4, 5):
        turn_of[i] = first_sum(i, ring_of[i])

    core_f.wait_recv()
    s2f[...] = cond[...] + rcond[...]
    y_f = [
        rcopy(s2f.at[pl.ds((y + k) % ny * 2, 2)], ryf.at[k], s3_sem.at[2, k], r3_sem.at[2, k], *at_y(k))
        for k in range(1, ny)
    ]
    for i in range(4):
        second_sum(i, turn_of[i])
    z_b = start_z(0)
    for c in y_f:
        c.wait_recv()
    total = s2f[pl.ds(y * 2, 2)]
    for k in range(1, ny):
        total = total + ryf[k]
    sxf[...] = total
    eye = lax.broadcasted_iota(jnp.int32, (32, 128), 0) == lax.broadcasted_iota(jnp.int32, (32, 128), 1)
    emb_row = jnp.sum(jnp.where(eye, emb, 0.0), axis=0, keepdims=True)
    for half in range(2):
        sxf[half, 2:3, 0:128] = emb_row
    x_f = [
        rcopy(sxf.at[(x + k) % 4 // 2], rxf.at[k], s3_sem.at[3, k], r3_sem.at[3, k], *at_x(k)) for k in range(1, 4)
    ]
    for i in (6, 7):
        turn_of[i] = first_sum(i, ring_of[i])
    for c in x_f:
        c.wait_recv()
    own = sxf[x // 2]
    first_row = lax.broadcasted_iota(jnp.int32, own.shape, 0) < 2
    s3f[0] = own + jnp.where(first_row, rxf[2], 0.0)
    s3f[1] = rxf[1] + jnp.where(first_row, rxf[3], 0.0)
    z_f = [rcopy(s3f, r3f.at[k], s3_sem.at[4, k], r3_sem.at[4, k], *at_z(k)) for k in range(1, nz)]
    for i in range(4, 8):
        second_sum(i, turn_of[i])
    z_a = start_z(1)

    for c in z_f:
        c.wait_recv()
    films = [None] * LAYERS
    for k in range(nz):
        for member in range(2):
            tile = s3f[member] if k == 0 else r3f[k, member]
            column = jnp.sum(jnp.where(eye, tile[2:3, 0:128], 0.0), axis=1, keepdims=True)
            for layer in range(LAYERS):
                part = column * tile[layer:layer + 1]
                films[layer] = part if films[layer] is None else films[layer] + part
    half = 2 * D // nm
    for layer in range(LAYERS):
        gf_ref[layer] = jnp.where(core == 0, films[layer][:, :half], films[layer][:, half:])
    z_sum(0, z_b, 1)
    z_sum(1, z_a, 0)

    for pair in (h_x1, h_nl, h_cot, h_x2, (up_a, up_b)):
        sent.extend(pair)
    sent.extend([core_of[i] for i in range(8)] + [core_f])
    for group in [g[i] for g in (ring_of, turn_of) for i in range(8)] + [y_f, x_f, z_f, z_a, z_b]:
        sent.extend(group)
    for c in sent:
        c.wait_send()


def hand_over(a_ref, b_ref, c_ref, a_out, b_out, c_out):
    a_out[...] = a_ref[...]
    b_out[...] = b_ref[...]
    c_out[...] = c_ref[...]


def body(ne, nm, inputs, cotangent, noise_level, neighbours, live_slots, projections, film_weights):
    emb = noise_features(noise_level)[0]
    emb = jnp.broadcast_to(emb[:, None], (2 * NOISE_FREQ, 128))
    nq, cw, rw, fl = nm // 2, D // nm, D // ne, 4 * D // nm
    ny, nz = nm // 4, ne // 2
    own = 2 * REACH
    vm = pl.BlockSpec(memory_space=pltpu.VMEM)
    V = pltpu.VMEM
    scratch = [
        V((LAYERS, 4, D, D), BF16),
        V((2, REACH, D), BF16), V((2, REACH, D), BF16), V((2, REACH, D), BF16), V((2, REACH, D), BF16),
        V((own, D), BF16), V((own, D), BF16),
        V((LAYERS, own, D), BF16), V((LAYERS, own, D), F32), V((LAYERS, own, 128), F32),
        V((LAYERS, 2 * own, D), BF16), V((LAYERS, 2 * own, D), BF16), V((LAYERS, 2 * own, D), BF16),
        V((2 * own, D), BF16),
        V((LAYERS, 2 * HEADS, REACH, WIN), F32), V((LAYERS, own, D), BF16),
        V((2, REACH, WIN), F32), V((2, REACH, WIN), F32),
        V((2, 32, 128), F32), V((2, 32, 128), F32),
        V((LAYERS, own, 128), F32), V((LAYERS, 2, 8, 128), F32), V((LAYERS, 2, 8, 128), F32),
        V((own, D), BF16), V((own, D), BF16), V((own, D), BF16),
        V((2 * HEADS, REACH, WIN), F32), V((2 * HEADS, REACH, WIN), F32),
        V((2 * HEADS, REACH, WIN), BF16), V((2 * HEADS, REACH, WIN), BF16),
        V((2, REACH, D), BF16), V((REACH, D), F32),
        V((8, 2, 4 * ny, cw, 256), BF16), V((8, 4 * ny, cw, 256), BF16),
        V((8, 4 * ny, cw, 256), BF16), V((8, 4, 4, cw, 256), BF16),
        V((8, 4, cw, 256), BF16), V((8, 4, cw, 256), BF16),
        V((2, 4 * cw, 256), F32), V((2, nz, rw, 4 * cw), BF16), V((2, nz, rw, 4 * cw), BF16),
        V((nq, 8, fl), F32), V((nq, 8, fl), F32), V((nq, 8, fl), F32), V((ny, 2, 8, fl), F32),
        V((2, 8, fl), F32), V((4, 8, fl), F32), V((2, 8, fl), F32), V((nz, 2, 8, fl), F32),
        pltpu.SemaphoreType.DMA((LAYERS, 4)),
        pltpu.SemaphoreType.DMA((7, 2)), pltpu.SemaphoreType.DMA((7, 2)),
        pltpu.SemaphoreType.DMA((9,)), pltpu.SemaphoreType.DMA((9,)),
        pltpu.SemaphoreType.DMA((8, 4)), pltpu.SemaphoreType.DMA((8, 4)),
        pltpu.SemaphoreType.DMA((8, 4)), pltpu.SemaphoreType.DMA((8, 4)),
        pltpu.SemaphoreType.DMA((5, 8)), pltpu.SemaphoreType.DMA((5, 8)),
    ]
    outs = pl.pallas_call(
        functools.partial(kernel, ne, nm),
        out_shape=(
            jax.ShapeDtypeStruct((1, own, D), BF16),
            jax.ShapeDtypeStruct((LAYERS, 4, rw, cw), F32),
            jax.ShapeDtypeStruct((LAYERS, 2 * NOISE_FREQ, fl // 2), F32),
        ),
        in_specs=[vm, vm, vm, vm, vm, pl.BlockSpec(memory_space=pl.ANY), vm],
        out_specs=(vm, vm, vm),
        scratch_shapes=scratch,
        compiler_params=pltpu.CompilerParams(
            collective_id=0, has_side_effects=True, vmem_limit_bytes=56 * 1024 * 1024
        ),
    )(inputs, cotangent, emb, neighbours.T, live_slots.T, projections, film_weights)
    return pl.pallas_call(
        hand_over,
        out_shape=tuple(jax.ShapeDtypeStruct(o.shape, o.dtype) for o in outs),
        in_specs=[vm, vm, vm],
        out_specs=(vm, vm, vm),
    )(*outs)


def solution(mesh):
    placed = (
        P("ens", "mesh", None),
        P("ens", "mesh", None),
        P("ens"),
        P("mesh", None),
        P("mesh", None),
        P(),
        P(),
    )
    return jax.shard_map(
        functools.partial(body, mesh.shape["ens"], mesh.shape["mesh"]),
        mesh=mesh,
        in_specs=placed,
        out_specs=(P("ens", "mesh", None), P(None, None, "ens", "mesh"), P(None, None, "mesh")),
        check_vma=False,
    )
```
